128 devices in a mesh: gx: 4 (over y_hi, core), gy: 4 (over z), ta: 8 (over x, y_lo).
Axes of the slice: x: 4, y: 4 (y_hi: 2, y_lo: 2; y = y_hi * 2 + y_lo), z: 4, core: 2. Of those that a mesh axis runs over, the one named last changes fastest.
Arguments:
- features: bfloat16 [32, 16, 16, 128, 256], P('ta', 'gx', 'gy'), may hold values from -6 to 6
- neighbours: int32 [16, 16, 4], P('gx', 'gy'), may hold values from 0 to 8, as said below
- adjacency: int32 [16, 16, 4, 128, 128], P('gx', 'gy'), may hold values 0 or 1
- w_space: bfloat16 [256, 256], replicated, may hold values from -0.375 to 0.375
- w_time: bfloat16 [3, 256, 256], replicated, may hold values from -0.21875 to 0.21875
- cotangent: bfloat16 [32, 16, 16, 128, 256], P('ta', 'gx', 'gy'), may hold values from -6 to 6
Outputs:
- updated: bfloat16 [32, 16, 16, 128, 256], P('ta', 'gx', 'gy')
- grad_space: float32 [256, 256], replicated
- grad_time: float32 [3, 256, 256], replicated
The draws below stay inside these ranges and needn't reach their ends.
Inputs may be any that keep to these rules, and one draw needn't show every extreme that they name: `neighbours`: the 4 codes of a tile are distinct; code c names the tile c // 3 - 1 tiles away along x and c % 3 - 1 tiles away along y, periodically.
All inputs are finite; a program needn't handle non-finite values. No bound on the sum of `adjacency` on one device may be relied on, other than what follows from the above.
Results may differ from the reference program's by a relative error of at most 0.0068.
Values may be sent and summed in bfloat16 or wider, within the bound.
No kernel may reach another device: no remote copies, remote signals or barrier semaphores. Data moves between devices by JAX's collectives and lax.ppermute only.
A program may use at most 128 MiB of HBM per device.

```python
import math
import jax
import jax.numpy as jnp
from jax import lax

WIDTH = 256
LIPIDS = 128
TAPS = 3
SLOTS = 4
TILES_X = 16
TILES_Y = 16
FRAMES = 32


def draw_neighbours(key, part):
    scores = jax.random.randint(key, (TILES_X, TILES_Y, 9), 0, 1 << 20, dtype=jnp.int32) * 9
    scores = scores + jnp.arange(9, dtype=jnp.int32)
    return lax.top_k(scores, SLOTS)[1].astype(jnp.int32)


def with_ends(entries, own_key, smallest, largest):
    extent = entries.shape
    spot = [jax.random.randint(jax.random.fold_in(own_key, axis), (), 0, extent[axis]) for axis in range(len(extent))]
    entries = entries.at[tuple(spot)].set(smallest)
    longest = extent.index(max(extent))
    spot[longest] = (spot[longest] + 1) % extent[longest]
    return entries.at[tuple(spot)].set(largest)


def block_levels(stream_key, dims, pieces, least, top_value):
    def one(dim, parts):
        heights = jax.random.uniform(jax.random.fold_in(jax.random.fold_in(stream_key, 6), dim), (parts,), jnp.float32, least / len(pieces), top_value / len(pieces))
        return jnp.repeat(jnp.exp(heights), dims[dim] // parts).reshape((-1,) + (1,) * (len(dims) - dim - 1))

    loudness = one(*pieces[0])
    for cut in pieces[1:]:
        loudness = loudness * one(*cut)
    return loudness


def scatter_about(stream_key, shape, width, most, split=(), held_as=jnp.bfloat16):
    values = width * jax.random.normal(stream_key, shape, jnp.float32)
    if split:
        values = values * block_levels(stream_key, shape, split, -0.22, 0.18)
    return jnp.clip(values, -most, most).astype(held_as)


def setup_inputs(seed: int = 0) -> dict:
    keys = jax.random.split(jax.random.key(seed), 7)
    return {
        "features": scatter_about(keys[0], (FRAMES, TILES_X, TILES_Y, LIPIDS, WIDTH), 1.0, 6.0, ((0, 8), (1, 4), (2, 4))),
        "neighbours": draw_neighbours(jax.random.fold_in(keys[6], 71), 0),
        "adjacency": with_ends((jax.random.randint(keys[2], (TILES_X, TILES_Y, SLOTS, LIPIDS, LIPIDS), 0, 16) < 1).astype(jnp.int32), jax.random.fold_in(keys[2], 1), 0, 1),
        "w_space": scatter_about(keys[3], (WIDTH, WIDTH), WIDTH ** -0.5, 0.375),
        "w_time": scatter_about(keys[4], (TAPS, WIDTH, WIDTH), (WIDTH * TAPS) ** -0.5, 0.21875),
        "cotangent": scatter_about(keys[5], (FRAMES, TILES_X, TILES_Y, LIPIDS, WIDTH), 1.0, 6.0, ((0, 8), (1, 4), (2, 4))),
    }


def reference(features, neighbours, adjacency, w_space, w_time, cotangent):
    tile_count = TILES_X * TILES_Y
    row_count = tile_count * LIPIDS
    behind = TAPS - 1
    along_x = jnp.arange(TILES_X, dtype=jnp.int32)[:, None]
    along_y = jnp.arange(TILES_Y, dtype=jnp.int32)[None, :]
    sources = []
    for slot_pos in range(SLOTS):
        offset_code = neighbours[:, :, slot_pos]
        source_x = (along_x + offset_code // 3 - 1) % TILES_X
        source_y = (along_y + offset_code % 3 - 1) % TILES_Y
        sources.append((source_x * TILES_Y + source_y).reshape(-1).astype(jnp.int32))
    lipid_masks = adjacency.reshape(tile_count, SLOTS, LIPIDS, LIPIDS).astype(jnp.float32)

    def spatial(one_frame):
        flat_tiles = one_frame.reshape(tile_count, LIPIDS, WIDTH).astype(jnp.float32)
        summed = jnp.zeros((tile_count, LIPIDS, WIDTH), jnp.float32)
        for slot_pos in range(SLOTS):
            picked = jnp.take(flat_tiles, sources[slot_pos], axis=0)
            summed = summed + jnp.einsum('tij,tjc->tic', lipid_masks[:, slot_pos], picked)
        return (0.18 * summed).astype(jnp.bfloat16).reshape(row_count, WIDTH)
    aggregate = lax.map(spatial, features)

    def project(block):
        return jnp.dot(block, w_space, preferred_element_type=jnp.float32).astype(jnp.bfloat16)
    projected = lax.map(project, aggregate)
    padded = jnp.concatenate([jnp.zeros((behind, row_count, WIDTH), jnp.bfloat16), projected], axis=0)
    flat_feats = features.reshape(FRAMES, row_count, WIDTH)
    flat_cot = cotangent.reshape(FRAMES, row_count, WIDTH)

    def forward(step_idx):
        mixed = jnp.zeros((row_count, WIDTH), jnp.float32)
        for offset in range(TAPS):
            earlier = lax.dynamic_index_in_dim(padded, step_idx + behind - offset, 0, keepdims=False)
            mixed = mixed + jnp.dot(earlier, w_time[offset], preferred_element_type=jnp.float32)
        sigmoid_z = jax.nn.sigmoid(mixed)
        own = lax.dynamic_index_in_dim(flat_feats, step_idx, 0, keepdims=False).astype(jnp.float32)
        result = (own + mixed * sigmoid_z).astype(jnp.bfloat16)
        grad_in = lax.dynamic_index_in_dim(flat_cot, step_idx, 0, keepdims=False).astype(jnp.float32)
        grad_mixed = (grad_in * sigmoid_z * (1.0 + mixed * (1.0 - sigmoid_z))).astype(jnp.bfloat16)
        return (result, grad_mixed)
    updated, grad_mixed = lax.map(forward, jnp.arange(FRAMES, dtype=jnp.int32))
    grad_padded = jnp.concatenate([grad_mixed, jnp.zeros((behind, row_count, WIDTH), jnp.bfloat16)], axis=0)

    def backward(carry, step_idx):
        space_sum, time_sum = carry
        grad_proj = jnp.zeros((row_count, WIDTH), jnp.float32)
        proj_now = lax.dynamic_index_in_dim(projected, step_idx, 0, keepdims=False)
        time_parts = []
        for offset in range(TAPS):
            later = lax.dynamic_index_in_dim(grad_padded, step_idx + offset, 0, keepdims=False)
            grad_proj = grad_proj + jnp.dot(later, w_time[offset].T, preferred_element_type=jnp.float32)
            time_parts.append(jnp.dot(proj_now.T, later, preferred_element_type=jnp.float32))
        grad_proj = grad_proj.astype(jnp.bfloat16)
        agg_now = lax.dynamic_index_in_dim(aggregate, step_idx, 0, keepdims=False)
        space_sum = space_sum + jnp.dot(agg_now.T, grad_proj, preferred_element_type=jnp.float32)
        time_sum = time_sum + jnp.stack(time_parts)
        return ((space_sum, time_sum), None)
    start = (jnp.zeros((WIDTH, WIDTH), jnp.float32), jnp.zeros((TAPS, WIDTH, WIDTH), jnp.float32))
    (space_sum, time_sum), unused = lax.scan(backward, start, jnp.arange(FRAMES, dtype=jnp.int32))
    row_scale = 1.0 / math.sqrt(FRAMES * row_count)
    updated = updated.reshape(FRAMES, TILES_X, TILES_Y, LIPIDS, WIDTH)
    return (updated, space_sum * row_scale, time_sum * row_scale)
```

```python
import functools
import math

import jax
import jax.numpy as jnp
import numpy as np
from jax import lax
from jax.experimental import pallas as pl
from jax.experimental.pallas import tpu as pltpu
from jax.sharding import Mesh
from jax.sharding import PartitionSpec as P

BF16 = jnp.bfloat16
F32 = jnp.float32
GX = ("yh", "core")
EVERY = ("yh", "core", "gy", "ta")


def ring(count, step):
    return [(i, (i + step) % count) for i in range(count)]


def whole_vmem():
    return pl.BlockSpec(memory_space=pltpu.VMEM)


def prep_kernel(adj_ref, ws_ref, wt_ref, mask_ref, v_ref):
    slots, lipids = adj_ref.shape[1], adj_ref.shape[2]
    width = ws_ref.shape[1]
    for k in range(slots):
        mask_ref[0, :, k * lipids : (k + 1) * lipids] = (
            adj_ref[0, k].astype(F32).astype(BF16)
        )

    @pl.when(pl.program_id(0) == 0)
    def _():
        for j in range(wt_ref.shape[0]):
            v_ref[j * width : (j + 1) * width, :] = jnp.dot(
                ws_ref[...], wt_ref[j], preferred_element_type=F32
            ).astype(BF16)


def prep(adjacency, w_space, w_time):
    tiles, slots, lipids, _ = adjacency.shape
    taps, width, _ = w_time.shape
    return pl.pallas_call(
        prep_kernel,
        grid=(tiles,),
        in_specs=[
            pl.BlockSpec((1, slots, lipids, lipids), lambda i: (i, 0, 0, 0)),
            pl.BlockSpec((width, width), lambda i: (0, 0)),
            pl.BlockSpec((taps, width, width), lambda i: (0, 0, 0)),
        ],
        out_specs=[
            pl.BlockSpec((1, lipids, slots * lipids), lambda i: (i, 0, 0)),
            pl.BlockSpec((taps * width, width), lambda i: (0, 0)),
        ],
        out_shape=[
            jax.ShapeDtypeStruct((tiles, lipids, slots * lipids), BF16),
            jax.ShapeDtypeStruct((taps * width, width), BF16),
        ],
        cost_estimate=pl.CostEstimate(
            flops=2 * taps * width**3, bytes_accessed=8 << 20, transcendentals=0
        ),
        name="prep",
    )(adjacency, w_space, w_time)


def agg_kernel(
    first, codes, feat, xlo, xhi, ylo, yhi, clo, chi, mask_ref, out_ref, ext, sems
):
    frames, nx, ny = out_ref.shape[:3]
    own = feat.at[pl.ds(first, frames)]
    moves = [
        (own, ext.at[:, 1 : nx + 1, 1 : ny + 1]),
        (xlo, ext.at[:, 0:1, 1 : ny + 1]),
        (xhi, ext.at[:, nx + 1 : nx + 2, 1 : ny + 1]),
        (ylo, ext.at[:, 1 : nx + 1, 0:1]),
        (yhi, ext.at[:, 1 : nx + 1, ny + 1 : ny + 2]),
        (clo.at[:, 0:1], ext.at[:, 0:1, 0:1]),
        (clo.at[:, 1:2], ext.at[:, nx + 1 : nx + 2, 0:1]),
        (chi.at[:, 0:1], ext.at[:, 0:1, ny + 1 : ny + 2]),
        (chi.at[:, 1:2], ext.at[:, nx + 1 : nx + 2, ny + 1 : ny + 2]),
    ]
    copies = [
        pltpu.make_async_copy(src, dst, sems.at[i]) for i, (src, dst) in enumerate(moves)
    ]
    for copy in copies:
        copy.start()
    for copy in copies:
        copy.wait()
    slots = mask_ref.shape[2] // mask_ref.shape[1]
    for x in range(nx):
        for y in range(ny):
            tile = x * ny + y
            places = []
            for k in range(slots):
                code = codes[tile * slots + k]
                places.append((x + lax.div(code, 3), y + lax.rem(code, 3)))
            mask = mask_ref[tile]
            for f in range(frames):
                source = jnp.concatenate([ext[f, sx, sy] for sx, sy in places], axis=0)
                summed = jnp.dot(mask, source, preferred_element_type=F32)
                out_ref[f, x, y] = (0.18 * summed).astype(BF16)


def aggregate(first, frames, codes, features, halo, mask):
    _, nx, ny, lipids, width = features.shape
    anywhere = pl.BlockSpec(memory_space=pl.ANY)
    flops = 2 * frames * nx * ny * lipids * mask.shape[2] * width
    return pl.pallas_call(
        functools.partial(agg_kernel, first),
        in_specs=[pl.BlockSpec(memory_space=pltpu.SMEM)] + [anywhere] * 7 + [whole_vmem()],
        out_specs=whole_vmem(),
        out_shape=jax.ShapeDtypeStruct((frames, nx, ny, lipids, width), BF16),
        scratch_shapes=[
            pltpu.VMEM((frames, nx + 2, ny + 2, lipids, width), BF16),
            pltpu.SemaphoreType.DMA((9,)),
        ],
        compiler_params=pltpu.CompilerParams(vmem_limit_bytes=40 << 20),
        cost_estimate=pl.CostEstimate(
            flops=flops, bytes_accessed=12 << 20, transcendentals=0
        ),
        name="aggregate",
    )(codes, features, *halo, mask)


def mix_kernel(p_ref, q_ref, feat_ref, cot_ref, v_ref, *rest):
    *given, up_ref, g_ref = rest

    @pl.when(pl.program_id(0) == 0)
    def _():
        g_ref[...] = given[0][...] if given else jnp.zeros_like(g_ref)

    before = [p_ref[0], p_ref[1], q_ref[0], q_ref[1]]
    rows, grads = [], []
    for f in range(2):
        left = jnp.concatenate([before[f + 2], before[f + 1], before[f]], axis=1)
        mixed = jnp.dot(left, v_ref[...], preferred_element_type=F32)
        s = 0.5 * jnp.tanh(0.5 * mixed) + 0.5
        up_ref[f] = (feat_ref[f].astype(F32) + mixed * s).astype(BF16)
        grad = cot_ref[f].astype(F32) * s * (1.0 + mixed * (1.0 - s))
        rows.append(left)
        grads.append(grad.astype(BF16))
    left = jnp.concatenate(rows, axis=0)
    grad = jnp.concatenate(grads, axis=0)
    g_ref[...] += lax.dot_general(
        left, grad, (((0,), (0,)), ((), ())), preferred_element_type=F32
    )


def mix(half, prev, now, features, cotangent, v, given=()):
    frames, count, width = now.shape
    rows = 512
    taps = v.shape[0] // width
    pair = pl.BlockSpec((frames, rows, width), lambda i: (0, i, 0))
    here = pl.BlockSpec((frames, rows, width), lambda i: (half, i, 0))
    full_v = pl.BlockSpec((taps * width, width), lambda i: (0, 0))
    return pl.pallas_call(
        mix_kernel,
        grid=(count // rows,),
        in_specs=[pair, pair, here, here, full_v]
        + ([full_v, pl.BlockSpec(memory_space=pl.ANY)] if given else []),
        out_specs=[here, full_v],
        out_shape=[
            jax.ShapeDtypeStruct(features.shape, BF16),
            jax.ShapeDtypeStruct((taps * width, width), F32),
        ],
        input_output_aliases={6: 0} if given else {},
        compiler_params=pltpu.CompilerParams(vmem_limit_bytes=40 << 20),
        cost_estimate=pl.CostEstimate(
            flops=4 * frames * count * taps * width * width,
            bytes_accessed=10 << 20,
            transcendentals=frames * count * width,
        ),
        name="mix",
    )(prev, now, features, cotangent, v, *given)


def finish_kernel(scale, g_ref, ws_ref, wt_ref, space_ref, time_ref):
    width = ws_ref.shape[0]
    space = jnp.zeros((width, width), F32)
    for j in range(wt_ref.shape[0]):
        g = g_ref[j * width : (j + 1) * width, :]
        high = g.astype(BF16)
        low = (g - high.astype(F32)).astype(BF16)
        time = 0.0
        for part in (low, high):
            time = time + lax.dot_general(
                ws_ref[...], part, (((0,), (0,)), ((), ())), preferred_element_type=F32
            )
            space = space + lax.dot_general(
                part, wt_ref[j], (((1,), (1,)), ((), ())), preferred_element_type=F32
            )
        time_ref[j] = time * scale
    space_ref[...] = space * scale


def finish(scale, total, w_space, w_time):
    return pl.pallas_call(
        functools.partial(finish_kernel, scale),
        in_specs=[whole_vmem()] * 3,
        out_specs=[whole_vmem()] * 2,
        out_shape=[
            jax.ShapeDtypeStruct(w_space.shape, F32),
            jax.ShapeDtypeStruct(w_time.shape, F32),
        ],
        name="finish",
    )(total, w_space, w_time)


def halo_of(part, nx, ny):
    x_up, x_down = ring(4, 1), ring(4, -1)
    xlo = lax.ppermute(part[:, nx - 1 :], GX, x_up)
    xhi = lax.ppermute(part[:, :1], GX, x_down)
    ylo = lax.ppermute(part[:, :, ny - 1 :], "gy", x_up)
    yhi = lax.ppermute(part[:, :, :1], "gy", x_down)
    clo = lax.ppermute(
        jnp.concatenate([xlo[:, :, ny - 1 :], xhi[:, :, ny - 1 :]], axis=1), "gy", x_up
    )
    chi = lax.ppermute(
        jnp.concatenate([xlo[:, :, :1], xhi[:, :, :1]], axis=1), "gy", x_down
    )
    return xlo, xhi, ylo, yhi, clo, chi


def all_sum(total):
    rows, width = total.shape
    count = lax.axis_size(EVERY)
    block = 8
    padded = jnp.pad(total, ((0, count * block - rows), (0, 0)))
    mine = lax.all_to_all(
        padded.reshape(count, block, width), EVERY, 0, 0, tiled=True
    ).sum(axis=0)
    spread = jnp.broadcast_to(mine[None], (count, block, width))
    back = lax.all_to_all(spread, EVERY, 0, 0, tiled=True)
    return back.reshape(count * block, width)[:rows]


def shards(features, neighbours, adjacency, w_space, w_time, cotangent):
    frames, nx, ny, lipids, width = features.shape
    count = nx * ny * lipids
    codes = neighbours.reshape(-1)
    halo_b = halo_of(features[2:4], nx, ny)
    halo_a = halo_of(features[0:2], nx, ny)
    mask, v = prep(adjacency.reshape(nx * ny, -1, lipids, lipids), w_space, w_time)
    agg_b = aggregate(2, 2, codes, features, halo_b, mask).reshape(2, count, width)
    prev = lax.ppermute(agg_b, "ta", [(i, i + 1) for i in range(7)])
    agg_a = aggregate(0, 2, codes, features, halo_a, mask).reshape(2, count, width)
    feat = features.reshape(frames, count, width)
    cot = cotangent.reshape(frames, count, width)
    updated, total = mix(1, agg_a, agg_b, feat, cot, v)
    updated, total = mix(0, prev, agg_a, feat, cot, v, (total, updated))
    total = all_sum(total)
    scale = 1.0 / math.sqrt(frames * count * lax.axis_size(EVERY))
    grad_space, grad_time = finish(scale, total, w_space, w_time)
    return updated.reshape(features.shape), grad_space, grad_time


def solution(mesh):
    gx, gy, ta = (mesh.shape[a] for a in ("gx", "gy", "ta"))
    fine = Mesh(
        np.asarray(mesh.devices).reshape(2, gx // 2, gy, ta), ("yh", "core", "gy", "ta")
    )
    in_specs = (
        P("ta", GX, "gy", None, None),
        P(GX, "gy", None),
        P(GX, "gy", None, None, None),
        P(),
        P(),
        P("ta", GX, "gy", None, None),
    )
    out_specs = (P("ta", GX, "gy", None, None), P(), P())
    return jax.shard_map(shards, mesh=fine, in_specs=in_specs, out_specs=out_specs, check_vma=False)
```

```python
import functools
import math

import jax
import jax.numpy as jnp
import numpy as np
from jax import lax
from jax.experimental import pallas as pl
from jax.experimental.pallas import tpu as pltpu
from jax.sharding import Mesh
from jax.sharding import PartitionSpec as P

BF16 = jnp.bfloat16
F32 = jnp.float32
GX = ("yh", "core")
MIX_ROWS = 512
VMEM = 20 << 20
EVERY = ("yh", "core", "gy", "ta")
REST = ("yh", "gy", "ta")


def ring(count, step):
    return [(i, (i + step) % count) for i in range(count)]


def whole_vmem():
    return pl.BlockSpec(memory_space=pltpu.VMEM)


def prep_kernel(adj_ref, ws_ref, wt_ref, mask_ref, v_ref):
    slots, lipids = adj_ref.shape[1], adj_ref.shape[2]
    width = ws_ref.shape[1]
    for t in range(adj_ref.shape[0]):
        for k in range(slots):
            mask_ref[t, :, k * lipids : (k + 1) * lipids] = (
                adj_ref[t, k].astype(F32).astype(BF16)
            )

    @pl.when(pl.program_id(0) == 0)
    def _():
        for j in range(wt_ref.shape[0]):
            v_ref[j * width : (j + 1) * width, :] = jnp.dot(
                ws_ref[...], wt_ref[j], preferred_element_type=F32
            ).astype(BF16)


def prep(adjacency, w_space, w_time):
    tiles, slots, lipids, _ = adjacency.shape
    taps, width, _ = w_time.shape
    return pl.pallas_call(
        prep_kernel,
        grid=(tiles // 4,),
        in_specs=[
            pl.BlockSpec((4, slots, lipids, lipids), lambda i: (i, 0, 0, 0)),
            pl.BlockSpec((width, width), lambda i: (0, 0)),
            pl.BlockSpec((taps, width, width), lambda i: (0, 0, 0)),
        ],
        out_specs=[
            pl.BlockSpec((4, lipids, slots * lipids), lambda i: (i, 0, 0)),
            pl.BlockSpec((taps * width, width), lambda i: (0, 0)),
        ],
        out_shape=[
            jax.ShapeDtypeStruct((tiles, lipids, slots * lipids), BF16),
            jax.ShapeDtypeStruct((taps * width, width), BF16),
        ],
        compiler_params=pltpu.CompilerParams(vmem_limit_bytes=VMEM),
        cost_estimate=pl.CostEstimate(
            flops=2 * taps * width**3, bytes_accessed=8 << 20, transcendentals=0
        ),
        name="prep",
    )(adjacency, w_space, w_time)


def pack_kernel(moves, count, *refs):
    *arrays, sems = refs
    copies = [
        pltpu.make_async_copy(arrays[i].at[src], arrays[count + o].at[dst], sems.at[n])
        for n, (i, src, o, dst) in enumerate(moves)
    ]
    for copy in copies:
        copy.start()
    for copy in copies:
        copy.wait()


def pack(arrays, shapes, moves):
    anywhere = pl.BlockSpec(memory_space=pl.ANY)
    return pl.pallas_call(
        functools.partial(pack_kernel, moves, len(arrays)),
        in_specs=[anywhere] * len(arrays),
        out_specs=[anywhere] * len(shapes),
        out_shape=[jax.ShapeDtypeStruct(shape, BF16) for shape in shapes],
        scratch_shapes=[pltpu.SemaphoreType.DMA((len(moves),))],
        compiler_params=pltpu.CompilerParams(vmem_limit_bytes=VMEM),
        cost_estimate=pl.CostEstimate(flops=0, bytes_accessed=6 << 20, transcendentals=0),
        name="pack",
    )(*arrays)


def agg_kernel(first, xs, edge, codes, feat, *rest):
    *halo, mask_hbm, out_ref, ext, mask_ref, sems = rest
    frames, _, ny = out_ref.shape[:3]
    nx = feat.shape[1]
    span = pl.ds(first, frames)
    moves = [
        (feat.at[span], ext.at[:, edge : nx + edge, 1 : ny + 1]),
        (halo[0], ext.at[:, edge : nx + edge, 0:1]),
        (halo[1], ext.at[:, edge : nx + edge, ny + 1 : ny + 2]),
    ] + [
        (mask_hbm.at[x * ny : (x + 1) * ny], mask_ref.at[i * ny : (i + 1) * ny])
        for i, x in enumerate(xs)
    ]
    if edge:
        xlo, xhi, clo, chi = (ref.at[span] for ref in halo[2:])
        moves += [
            (xlo, ext.at[:, 0:1, 1 : ny + 1]),
            (xhi, ext.at[:, nx + 1 : nx + 2, 1 : ny + 1]),
            (clo.at[:, 0:1], ext.at[:, 0:1, 0:1]),
            (clo.at[:, 1:2], ext.at[:, nx + 1 : nx + 2, 0:1]),
            (chi.at[:, 0:1], ext.at[:, 0:1, ny + 1 : ny + 2]),
            (chi.at[:, 1:2], ext.at[:, nx + 1 : nx + 2, ny + 1 : ny + 2]),
        ]
    copies = [
        pltpu.make_async_copy(src, dst, sems.at[i]) for i, (src, dst) in enumerate(moves)
    ]
    for copy in copies:
        copy.start()
    for copy in copies:
        copy.wait()
    slots = mask_ref.shape[2] // mask_ref.shape[1]
    for i, x in enumerate(xs):
        for y in range(ny):
            tile = x * ny + y
            places = []
            for k in range(slots):
                code = codes[tile * slots + k]
                places.append((x - 1 + edge + lax.div(code, 3), y + lax.rem(code, 3)))
            mask = mask_ref[i * ny + y]
            for f in range(frames):
                source = jnp.concatenate([ext[f, sx, sy] for sx, sy in places], axis=0)
                summed = jnp.dot(mask, source, preferred_element_type=F32)
                out_ref[f, i, y] = (0.18 * summed).astype(BF16)


def aggregate(first, xs, codes, features, halo, mask):
    _, nx, ny, lipids, width = features.shape
    frames = 2
    slots = mask.shape[2] // lipids
    edge = 1 if len(halo) > 2 else 0
    anywhere = pl.BlockSpec(memory_space=pl.ANY)
    flops = 2 * frames * len(xs) * ny * lipids * mask.shape[2] * width
    out = pl.pallas_call(
        functools.partial(agg_kernel, first, xs, edge),
        in_specs=[
            pl.BlockSpec(memory_space=pltpu.SMEM),
            pl.BlockSpec(memory_space=pltpu.HBM),
        ]
        + [anywhere] * (len(halo) + 1),
        out_specs=whole_vmem(),
        out_shape=jax.ShapeDtypeStruct((frames, len(xs), ny, lipids, width), BF16),
        scratch_shapes=[
            pltpu.VMEM((frames, nx + 2 * edge, ny + 2, lipids, width), BF16),
            pltpu.VMEM((len(xs) * ny, lipids, slots * lipids), BF16),
            pltpu.SemaphoreType.DMA((9 + len(xs),)),
        ],
        compiler_params=pltpu.CompilerParams(vmem_limit_bytes=VMEM),
        cost_estimate=pl.CostEstimate(
            flops=flops, bytes_accessed=8 << 20, transcendentals=0
        ),
        name="aggregate",
    )(codes, features, *halo, mask)
    return out.reshape(frames, -1, width)


def mix_kernel(p_ref, q_ref, feat_ref, cot_ref, v_ref, *rest):
    *given, up_ref, g_ref = rest

    @pl.when(pl.program_id(0) == 0)
    def _():
        g_ref[...] = given[0][...] if given else jnp.zeros_like(g_ref)

    before = [p_ref[0], p_ref[1], q_ref[0], q_ref[1]]
    rows, grads = [], []
    for f in range(2):
        left = jnp.concatenate([before[f + 2], before[f + 1], before[f]], axis=1)
        mixed = jnp.dot(left, v_ref[...], preferred_element_type=F32)
        s = 0.5 * jnp.tanh(0.5 * mixed) + 0.5
        up_ref[f] = (feat_ref[f].astype(F32) + mixed * s).astype(BF16)
        grad = cot_ref[f].astype(F32) * s * (1.0 + mixed * (1.0 - s))
        rows.append(left)
        grads.append(grad.astype(BF16))
    left = jnp.concatenate(rows, axis=0)
    grad = jnp.concatenate(grads, axis=0)
    g_ref[...] += lax.dot_general(
        left, grad, (((0,), (0,)), ((), ())), preferred_element_type=F32
    )


def mix(half, place, prev, now, features, cotangent, v, given=()):
    frames, count, width = now.shape
    rows = MIX_ROWS
    taps = v.shape[0] // width
    pair = pl.BlockSpec((frames, rows, width), lambda i: (0, i, 0))
    here = pl.BlockSpec((frames, rows, width), lambda i: (half, place(i), 0))
    full_v = pl.BlockSpec((taps * width, width), lambda i: (0, 0))
    return pl.pallas_call(
        mix_kernel,
        grid=(count // rows,),
        in_specs=[pair, pair, here, here, full_v]
        + ([full_v, pl.BlockSpec(memory_space=pl.ANY)] if given else []),
        out_specs=[here, full_v],
        out_shape=[
            jax.ShapeDtypeStruct(features.shape, BF16),
            jax.ShapeDtypeStruct((taps * width, width), F32),
        ],
        input_output_aliases={6: 0} if given else {},
        compiler_params=pltpu.CompilerParams(vmem_limit_bytes=VMEM),
        cost_estimate=pl.CostEstimate(
            flops=4 * frames * count * taps * width * width,
            bytes_accessed=10 << 20,
            transcendentals=frames * count * width,
        ),
        name="mix",
    )(prev, now, features, cotangent, v, *given)


def finish_kernel(scale, g_ref, ws_ref, wt_ref, space_ref, time_ref):
    width = ws_ref.shape[0]
    space = jnp.zeros((width, width), F32)
    for j in range(wt_ref.shape[0]):
        g = g_ref[j * width : (j + 1) * width, :]
        high = g.astype(BF16)
        low = (g - high.astype(F32)).astype(BF16)
        time = 0.0
        for part in (low, high):
            time = time + lax.dot_general(
                ws_ref[...], part, (((0,), (0,)), ((), ())), preferred_element_type=F32
            )
            space = space + lax.dot_general(
                part, wt_ref[j], (((1,), (1,)), ((), ())), preferred_element_type=F32
            )
        time_ref[j] = time * scale
    space_ref[...] = space * scale


def finish(scale, total, w_space, w_time):
    return pl.pallas_call(
        functools.partial(finish_kernel, scale),
        in_specs=[whole_vmem()] * 3,
        out_specs=[whole_vmem()] * 2,
        out_shape=[
            jax.ShapeDtypeStruct(w_space.shape, F32),
            jax.ShapeDtypeStruct(w_time.shape, F32),
        ],
        compiler_params=pltpu.CompilerParams(vmem_limit_bytes=VMEM),
        name="finish",
    )(total, w_space, w_time)


def all_sum(total):
    rows, width = total.shape
    half, block = rows // 2, 8
    count = lax.axis_size(REST)
    me = lax.axis_index("core")
    keep = lax.dynamic_slice_in_dim(total, me * half, half, 0)
    give = lax.dynamic_slice_in_dim(total, (1 - me) * half, half, 0)
    mine = keep + lax.ppermute(give, "core", ring(2, 1))
    mine = jnp.pad(mine, ((0, count * block - half), (0, 0)))
    mine = lax.all_to_all(mine.reshape(count, block, width), REST, 0, 0, tiled=True)
    spread = jnp.broadcast_to(mine.sum(axis=0)[None], (count, block, width))
    back = lax.all_to_all(spread, REST, 0, 0, tiled=True)
    back = back.reshape(count * block, width)[:half]
    other = lax.ppermute(back, "core", ring(2, 1))
    return jnp.where(
        me == 0, jnp.concatenate([back, other]), jnp.concatenate([other, back])
    )


def shards(features, neighbours, adjacency, w_space, w_time, cotangent):
    frames, nx, ny, lipids, width = features.shape
    count = nx * ny * lipids
    codes = neighbours.reshape(-1)
    up, down = ring(4, 1), ring(4, -1)
    onward = [(i, i + 1) for i in range(7)]
    inner, outer = tuple(range(1, nx - 1)), (0, nx - 1)

    y_edge, x_edge = (2, nx, 1, lipids, width), (frames, 1, ny, lipids, width)
    every = slice(None)
    low, high = slice(0, 1), slice(ny - 1, ny)

    def y_halo(high_edge, low_edge):
        return lax.ppermute(high_edge, "gy", up), lax.ppermute(low_edge, "gy", down)

    y_high, y_low, x_high, x_low = pack(
        [features],
        [y_edge, y_edge, x_edge, x_edge],
        [
            (0, (slice(2, 4), every, high), 0, ()),
            (0, (slice(2, 4), every, low), 1, ()),
            (0, (every, slice(nx - 1, nx)), 2, ()),
            (0, (every, low), 3, ()),
        ],
    )
    y_b = y_halo(y_high, y_low)
    xlo, xhi = lax.ppermute(x_high, GX, up), lax.ppermute(x_low, GX, down)
    mask, v = prep(adjacency.reshape(nx * ny, -1, lipids, lipids), w_space, w_time)
    inner_b = aggregate(2, inner, codes, features, y_b, mask)
    prev_inner = lax.ppermute(inner_b, "ta", onward)
    features_a, xlo, xhi, _ = lax.optimization_barrier((features, xlo, xhi, inner_b))
    y_a = y_halo(
        *pack(
            [features_a],
            [y_edge, y_edge],
            [
                (0, (slice(0, 2), every, high), 0, ()),
                (0, (slice(0, 2), every, low), 1, ()),
            ],
        )
    )
    corner = (frames, 2, 1, lipids, width)
    c_high, c_low = pack(
        [xlo, xhi],
        [corner, corner],
        [
            (i, (every, every, side), o, (every, slice(i, i + 1)))
            for i in range(2)
            for o, side in enumerate((high, low))
        ],
    )
    clo, chi = y_halo(c_high, c_low)
    rest = (xlo, xhi, clo, chi)
    outer_b = aggregate(2, outer, codes, features, (*y_b, *rest), mask)
    prev_outer = lax.ppermute(outer_b, "ta", onward)
    mask_a, _ = lax.optimization_barrier((mask, outer_b))
    inner_a = aggregate(0, inner, codes, features, y_a, mask_a)
    outer_a = aggregate(0, outer, codes, features, (*y_a, *rest), mask_a)
    feat = features.reshape(frames, count, width)
    cot = cotangent.reshape(frames, count, width)
    per_row = ny * lipids // MIX_ROWS

    def in_inner(i):
        return i + per_row

    def in_outer(i):
        return i + lax.div(i, per_row) * (nx - 2) * per_row

    updated, total = mix(1, in_inner, inner_a, inner_b, feat, cot, v)
    updated, total = mix(1, in_outer, outer_a, outer_b, feat, cot, v, (total, updated))
    updated, total = mix(0, in_inner, prev_inner, inner_a, feat, cot, v, (total, updated))
    updated, total = mix(0, in_outer, prev_outer, outer_a, feat, cot, v, (total, updated))
    total = all_sum(total)
    scale = 1.0 / math.sqrt(frames * count * lax.axis_size(EVERY))
    grad_space, grad_time = finish(scale, total, w_space, w_time)
    return updated.reshape(features.shape), grad_space, grad_time


def solution(mesh):
    gx, gy, ta = (mesh.shape[a] for a in ("gx", "gy", "ta"))
    fine = Mesh(
        np.asarray(mesh.devices).reshape(2, gx // 2, gy, ta), ("yh", "core", "gy", "ta")
    )
    in_specs = (
        P("ta", GX, "gy", None, None),
        P(GX, "gy", None),
        P(GX, "gy", None, None, None),
        P(),
        P(),
        P("ta", GX, "gy", None, None),
    )
    out_specs = (P("ta", GX, "gy", None, None), P(), P())
    return jax.shard_map(shards, mesh=fine, in_specs=in_specs, out_specs=out_specs, check_vma=False)
```

```python
import functools
import math

import jax
import jax.numpy as jnp
import numpy as np
from jax import lax
from jax.experimental import pallas as pl
from jax.experimental.pallas import tpu as pltpu
from jax.sharding import Mesh
from jax.sharding import PartitionSpec as P

BF16 = jnp.bfloat16
F32 = jnp.float32
GX = ("yh", "core")
MIX_ROWS = 512
VMEM = 65300 << 10
EVERY = ("yh", "core", "gy", "ta")
REST = ("yh", "gy", "ta")


def ring(count, step):
    return [(i, (i + step) % count) for i in range(count)]


def whole_vmem():
    return pl.BlockSpec(memory_space=pltpu.VMEM)


def prep_kernel(adj_ref, ws_ref, wt_ref, mask_ref, v_ref):
    slots, lipids = adj_ref.shape[1], adj_ref.shape[2]
    width = ws_ref.shape[1]
    for t in range(adj_ref.shape[0]):
        for k in range(slots):
            mask_ref[t, :, k * lipids : (k + 1) * lipids] = (
                adj_ref[t, k].astype(F32).astype(BF16)
            )

    @pl.when(pl.program_id(0) == 0)
    def _():
        for j in range(wt_ref.shape[0]):
            v_ref[j * width : (j + 1) * width, :] = jnp.dot(
                ws_ref[...], wt_ref[j], preferred_element_type=F32
            ).astype(BF16)


def prep(adjacency, w_space, w_time):
    tiles, slots, lipids, _ = adjacency.shape
    taps, width, _ = w_time.shape
    return pl.pallas_call(
        prep_kernel,
        grid=(tiles // 4,),
        in_specs=[
            pl.BlockSpec((4, slots, lipids, lipids), lambda i: (i, 0, 0, 0)),
            pl.BlockSpec((width, width), lambda i: (0, 0)),
            pl.BlockSpec((taps, width, width), lambda i: (0, 0, 0)),
        ],
        out_specs=[
            pl.BlockSpec((4, lipids, slots * lipids), lambda i: (i, 0, 0)),
            pl.BlockSpec((taps * width, width), lambda i: (0, 0)),
        ],
        out_shape=[
            jax.ShapeDtypeStruct((tiles, lipids, slots * lipids), BF16),
            jax.ShapeDtypeStruct((taps * width, width), BF16),
        ],
        compiler_params=pltpu.CompilerParams(vmem_limit_bytes=VMEM),
        cost_estimate=pl.CostEstimate(
            flops=2 * taps * width**3, bytes_accessed=8 << 20, transcendentals=0
        ),
        name="prep",
    )(adjacency, w_space, w_time)


def pack_kernel(moves, count, *refs):
    *arrays, sems = refs
    copies = [
        pltpu.make_async_copy(arrays[i].at[src], arrays[count + o].at[dst], sems.at[n])
        for n, (i, src, o, dst) in enumerate(moves)
    ]
    for copy in copies:
        copy.start()
    for copy in copies:
        copy.wait()


def pack(arrays, shapes, moves):
    anywhere = pl.BlockSpec(memory_space=pl.ANY)
    return pl.pallas_call(
        functools.partial(pack_kernel, moves, len(arrays)),
        in_specs=[anywhere] * len(arrays),
        out_specs=[anywhere] * len(shapes),
        out_shape=[jax.ShapeDtypeStruct(shape, BF16) for shape in shapes],
        scratch_shapes=[pltpu.SemaphoreType.DMA((len(moves),))],
        compiler_params=pltpu.CompilerParams(vmem_limit_bytes=VMEM),
        cost_estimate=pl.CostEstimate(flops=0, bytes_accessed=6 << 20, transcendentals=0),
        name="pack",
    )(*arrays)


def agg_kernel(first, xs, edge, codes, feat, *rest):
    *halo, mask_hbm, out_ref, ext, mask_ref, sems = rest
    frames, _, ny = out_ref.shape[:3]
    nx = feat.shape[1]
    span = pl.ds(first, frames)
    moves = [
        (feat.at[span], ext.at[:, edge : nx + edge, 1 : ny + 1]),
        (halo[0], ext.at[:, edge : nx + edge, 0:1]),
        (halo[1], ext.at[:, edge : nx + edge, ny + 1 : ny + 2]),
    ] + [
        (mask_hbm.at[x * ny : (x + 1) * ny], mask_ref.at[i * ny : (i + 1) * ny])
        for i, x in enumerate(xs)
    ]
    if edge:
        xlo, xhi, clo, chi = halo[2:]
        moves += [
            (xlo, ext.at[:, 0:1, 1 : ny + 1]),
            (xhi, ext.at[:, nx + 1 : nx + 2, 1 : ny + 1]),
            (clo.at[:, 0:1], ext.at[:, 0:1, 0:1]),
            (clo.at[:, 1:2], ext.at[:, nx + 1 : nx + 2, 0:1]),
            (chi.at[:, 0:1], ext.at[:, 0:1, ny + 1 : ny + 2]),
            (chi.at[:, 1:2], ext.at[:, nx + 1 : nx + 2, ny + 1 : ny + 2]),
        ]
    copies = [
        pltpu.make_async_copy(src, dst, sems.at[i]) for i, (src, dst) in enumerate(moves)
    ]
    for copy in copies:
        copy.start()
    for copy in copies:
        copy.wait()
    slots = mask_ref.shape[2] // mask_ref.shape[1]
    for i, x in enumerate(xs):
        for y in range(ny):
            tile = x * ny + y
            places = []
            for k in range(slots):
                code = codes[tile * slots + k]
                places.append((x - 1 + edge + lax.div(code, 3), y + lax.rem(code, 3)))
            mask = mask_ref[i * ny + y]
            for f in range(frames):
                source = jnp.concatenate([ext[f, sx, sy] for sx, sy in places], axis=0)
                summed = jnp.dot(mask, source, preferred_element_type=F32)
                out_ref[f, i, y] = (0.18 * summed).astype(BF16)


def aggregate(first, xs, codes, features, halo, mask):
    _, nx, ny, lipids, width = features.shape
    frames = 2
    slots = mask.shape[2] // lipids
    edge = 1 if len(halo) > 2 else 0
    anywhere = pl.BlockSpec(memory_space=pl.ANY)
    flops = 2 * frames * len(xs) * ny * lipids * mask.shape[2] * width
    out = pl.pallas_call(
        functools.partial(agg_kernel, first, xs, edge),
        in_specs=[
            pl.BlockSpec(memory_space=pltpu.SMEM),
            pl.BlockSpec(memory_space=pltpu.HBM),
        ]
        + [anywhere] * (len(halo) + 1),
        out_specs=whole_vmem(),
        out_shape=jax.ShapeDtypeStruct((frames, len(xs), ny, lipids, width), BF16),
        scratch_shapes=[
            pltpu.VMEM((frames, nx + 2 * edge, ny + 2, lipids, width), BF16),
            pltpu.VMEM((len(xs) * ny, lipids, slots * lipids), BF16),
            pltpu.SemaphoreType.DMA((9 + len(xs),)),
        ],
        compiler_params=pltpu.CompilerParams(vmem_limit_bytes=VMEM),
        cost_estimate=pl.CostEstimate(
            flops=flops, bytes_accessed=8 << 20, transcendentals=0
        ),
        name="aggregate",
    )(codes, features, *halo, mask)
    return out.reshape(frames, -1, width)


def mix_kernel(p_ref, q_ref, feat_ref, cot_ref, v_ref, *rest):
    *given, up_ref, g_ref = rest

    @pl.when(pl.program_id(0) == 0)
    def _():
        g_ref[...] = given[0][...] if given else jnp.zeros_like(g_ref)

    before = [p_ref[0], p_ref[1], q_ref[0], q_ref[1]]
    rows, grads = [], []
    for f in range(2):
        left = jnp.concatenate([before[f + 2], before[f + 1], before[f]], axis=1)
        mixed = jnp.dot(left, v_ref[...], preferred_element_type=F32)
        s = 0.5 * jnp.tanh(0.5 * mixed) + 0.5
        up_ref[f] = (feat_ref[f].astype(F32) + mixed * s).astype(BF16)
        grad = cot_ref[f].astype(F32) * s * (1.0 + mixed * (1.0 - s))
        rows.append(left)
        grads.append(grad.astype(BF16))
    left = jnp.concatenate(rows, axis=0)
    grad = jnp.concatenate(grads, axis=0)
    g_ref[...] += lax.dot_general(
        left, grad, (((0,), (0,)), ((), ())), preferred_element_type=F32
    )


def mix(half, place, prev, now, features, cotangent, v, given=()):
    frames, count, width = now.shape
    rows = MIX_ROWS
    taps = v.shape[0] // width
    pair = pl.BlockSpec((frames, rows, width), lambda i: (0, i, 0))
    here = pl.BlockSpec((frames, rows, width), lambda i: (half, place(i), 0))
    full_v = pl.BlockSpec((taps * width, width), lambda i: (0, 0))
    return pl.pallas_call(
        mix_kernel,
        grid=(count // rows,),
        in_specs=[pair, pair, here, here, full_v]
        + ([full_v, pl.BlockSpec(memory_space=pl.ANY)] if given else []),
        out_specs=[here, full_v],
        out_shape=[
            jax.ShapeDtypeStruct(features.shape, BF16),
            jax.ShapeDtypeStruct((taps * width, width), F32),
        ],
        input_output_aliases={6: 0} if given else {},
        compiler_params=pltpu.CompilerParams(vmem_limit_bytes=VMEM),
        cost_estimate=pl.CostEstimate(
            flops=4 * frames * count * taps * width * width,
            bytes_accessed=10 << 20,
            transcendentals=frames * count * width,
        ),
        name="mix",
    )(prev, now, features, cotangent, v, *given)


def finish_kernel(scale, g_ref, ws_ref, wt_ref, space_ref, time_ref):
    width = ws_ref.shape[0]
    space = jnp.zeros((width, width), F32)
    for j in range(wt_ref.shape[0]):
        g = g_ref[j * width : (j + 1) * width, :]
        high = g.astype(BF16)
        low = (g - high.astype(F32)).astype(BF16)
        time = 0.0
        for part in (low, high):
            time = time + lax.dot_general(
                ws_ref[...], part, (((0,), (0,)), ((), ())), preferred_element_type=F32
            )
            space = space + lax.dot_general(
                part, wt_ref[j], (((1,), (1,)), ((), ())), preferred_element_type=F32
            )
        time_ref[j] = time * scale
    space_ref[...] = space * scale


def finish(scale, total, w_space, w_time):
    return pl.pallas_call(
        functools.partial(finish_kernel, scale),
        in_specs=[whole_vmem()] * 3,
        out_specs=[whole_vmem()] * 2,
        out_shape=[
            jax.ShapeDtypeStruct(w_space.shape, F32),
            jax.ShapeDtypeStruct(w_time.shape, F32),
        ],
        compiler_params=pltpu.CompilerParams(vmem_limit_bytes=20 << 20),
        name="finish",
    )(total, w_space, w_time)


def all_sum(total):
    rows, width = total.shape
    half, block = rows // 2, 8
    count = lax.axis_size(REST)
    me = lax.axis_index("core")
    keep = lax.dynamic_slice_in_dim(total, me * half, half, 0)
    give = lax.dynamic_slice_in_dim(total, (1 - me) * half, half, 0)
    mine = keep + lax.ppermute(give, "core", ring(2, 1))
    mine = jnp.pad(mine, ((0, count * block - half), (0, 0)))
    mine = lax.all_to_all(mine.reshape(count, block, width), REST, 0, 0, tiled=True)
    spread = jnp.broadcast_to(mine.sum(axis=0)[None], (count, block, width))
    back = lax.all_to_all(spread, REST, 0, 0, tiled=True)
    back = back.reshape(count * block, width)[:half]
    other = lax.ppermute(back, "core", ring(2, 1))
    return jnp.where(
        me == 0, jnp.concatenate([back, other]), jnp.concatenate([other, back])
    )


def shards(features, neighbours, adjacency, w_space, w_time, cotangent):
    frames, nx, ny, lipids, width = features.shape
    count = nx * ny * lipids
    codes = neighbours.reshape(-1)
    up, down = ring(4, 1), ring(4, -1)
    onward = [(i, i + 1) for i in range(7)]
    inner, outer = tuple(range(1, nx - 1)), (0, nx - 1)

    every = slice(None)
    low, high = slice(0, 1), slice(ny - 1, ny)

    def exchange(axis, high_edge, low_edge):
        return lax.ppermute(high_edge, axis, up), lax.ppermute(low_edge, axis, down)

    def edges(first, source):
        pair = slice(first, first + 2)
        x_edge, y_edge = (2, 1, ny, lipids, width), (2, nx, 1, lipids, width)
        return pack(
            [source],
            [x_edge, x_edge, y_edge, y_edge],
            [
                (0, (pair, slice(nx - 1, nx)), 0, ()),
                (0, (pair, low), 1, ()),
                (0, (pair, every, high), 2, ()),
                (0, (pair, every, low), 3, ()),
            ],
        )

    def corners(x_halo):
        corner = (2, 2, 1, lipids, width)
        ends = pack(
            x_halo,
            [corner, corner],
            [
                (i, (every, every, side), o, (every, slice(i, i + 1)))
                for i in range(2)
                for o, side in enumerate((high, low))
            ],
        )
        return exchange("gy", *ends)

    edges_b = edges(2, features)
    x_b = exchange(GX, *edges_b[:2])
    y_b = exchange("gy", *edges_b[2:])
    mask, v = prep(adjacency.reshape(nx * ny, -1, lipids, lipids), w_space, w_time)
    later, _, _ = lax.optimization_barrier((features, edges_b, mask))
    edges_a = edges(0, later)
    x_a = exchange(GX, *edges_a[:2])
    y_a = exchange("gy", *edges_a[2:])
    c_b = corners(x_b)
    inner_b = aggregate(2, inner, codes, features, y_b, mask)
    prev_inner = lax.ppermute(inner_b, "ta", onward)
    c_b, _, _ = lax.optimization_barrier((c_b, inner_b, x_a))
    outer_b = aggregate(2, outer, codes, features, (*y_b, *x_b, *c_b), mask)
    prev_outer = lax.ppermute(outer_b, "ta", onward)
    x_a, y_a, mask_a, _ = lax.optimization_barrier((x_a, y_a, mask, outer_b))
    c_a = corners(x_a)
    inner_a = aggregate(0, inner, codes, features, y_a, mask_a)
    outer_a = aggregate(0, outer, codes, features, (*y_a, *x_a, *c_a), mask_a)
    feat = features.reshape(frames, count, width)
    cot = cotangent.reshape(frames, count, width)
    per_row = ny * lipids // MIX_ROWS

    def in_inner(i):
        return i + per_row

    def in_outer(i):
        return i + lax.div(i, per_row) * (nx - 2) * per_row

    updated, total = mix(1, in_inner, inner_a, inner_b, feat, cot, v)
    updated, total = mix(1, in_outer, outer_a, outer_b, feat, cot, v, (total, updated))
    updated, total = mix(0, in_inner, prev_inner, inner_a, feat, cot, v, (total, updated))
    updated, total = mix(0, in_outer, prev_outer, outer_a, feat, cot, v, (total, updated))
    total = all_sum(total)
    scale = 1.0 / math.sqrt(frames * count * lax.axis_size(EVERY))
    grad_space, grad_time = finish(scale, total, w_space, w_time)
    return updated.reshape(features.shape), grad_space, grad_time


def solution(mesh):
    gx, gy, ta = (mesh.shape[a] for a in ("gx", "gy", "ta"))
    fine = Mesh(
        np.asarray(mesh.devices).reshape(2, gx // 2, gy, ta), ("yh", "core", "gy", "ta")
    )
    in_specs = (
        P("ta", GX, "gy", None, None),
        P(GX, "gy", None),
        P(GX, "gy", None, None, None),
        P(),
        P(),
        P("ta", GX, "gy", None, None),
    )
    out_specs = (P("ta", GX, "gy", None, None), P(), P())
    return jax.shard_map(shards, mesh=fine, in_specs=in_specs, out_specs=out_specs, check_vma=False)
```

```python
import functools
import math

import jax
import jax.numpy as jnp
import numpy as np
from jax import lax
from jax.experimental import pallas as pl
from jax.experimental.pallas import tpu as pltpu
from jax.sharding import Mesh
from jax.sharding import PartitionSpec as P

BF16 = jnp.bfloat16
F32 = jnp.float32
GX = ("yh", "core")
MIX_ROWS = 256
VMEM = 65300 << 10
EVERY = ("yh", "core", "gy", "ta")
REST = ("yh", "gy", "ta")


def ring(count, step):
    return [(i, (i + step) % count) for i in range(count)]


def whole_vmem():
    return pl.BlockSpec(memory_space=pltpu.VMEM)


def prep_kernel(adj_ref, ws_ref, wt_ref, mask_ref, v_ref):
    slots, lipids = adj_ref.shape[1], adj_ref.shape[2]
    width = ws_ref.shape[1]
    for t in range(adj_ref.shape[0]):
        for k in range(slots):
            mask_ref[t, :, k * lipids : (k + 1) * lipids] = (
                adj_ref[t, k].astype(F32).astype(BF16)
            )

    @pl.when(pl.program_id(0) == 0)
    def _():
        for j in range(wt_ref.shape[0]):
            v_ref[j * width : (j + 1) * width, :] = jnp.dot(
                ws_ref[...], wt_ref[j], preferred_element_type=F32
            ).astype(BF16)


def prep(adjacency, w_space, w_time):
    tiles, slots, lipids, _ = adjacency.shape
    taps, width, _ = w_time.shape
    return pl.pallas_call(
        prep_kernel,
        grid=(tiles // 4,),
        in_specs=[
            pl.BlockSpec((4, slots, lipids, lipids), lambda i: (i, 0, 0, 0)),
            pl.BlockSpec((width, width), lambda i: (0, 0)),
            pl.BlockSpec((taps, width, width), lambda i: (0, 0, 0)),
        ],
        out_specs=[
            pl.BlockSpec((4, lipids, slots * lipids), lambda i: (i, 0, 0)),
            pl.BlockSpec((taps * width, width), lambda i: (0, 0)),
        ],
        out_shape=[
            jax.ShapeDtypeStruct((tiles, lipids, slots * lipids), BF16),
            jax.ShapeDtypeStruct((taps * width, width), BF16),
        ],
        compiler_params=pltpu.CompilerParams(vmem_limit_bytes=VMEM),
        cost_estimate=pl.CostEstimate(
            flops=2 * taps * width**3, bytes_accessed=8 << 20, transcendentals=0
        ),
        name="prep",
    )(adjacency, w_space, w_time)


def pack_kernel(moves, count, *refs):
    *arrays, sems = refs
    copies = [
        pltpu.make_async_copy(arrays[i].at[src], arrays[count + o].at[dst], sems.at[n])
        for n, (i, src, o, dst) in enumerate(moves)
    ]
    for copy in copies:
        copy.start()
    for copy in copies:
        copy.wait()


def pack(arrays, shapes, moves):
    anywhere = pl.BlockSpec(memory_space=pl.ANY)
    return pl.pallas_call(
        functools.partial(pack_kernel, moves, len(arrays)),
        in_specs=[anywhere] * len(arrays),
        out_specs=[whole_vmem()] * len(shapes),
        out_shape=[jax.ShapeDtypeStruct(shape, BF16) for shape in shapes],
        scratch_shapes=[pltpu.SemaphoreType.DMA((len(moves),))],
        compiler_params=pltpu.CompilerParams(vmem_limit_bytes=VMEM),
        cost_estimate=pl.CostEstimate(flops=0, bytes_accessed=6 << 20, transcendentals=0),
        name="pack",
    )(*arrays)


def agg_kernel(first, xs, edge, pieces, codes, feat, *rest):
    *ins, ext, mask_ref, out_ref, sems = rest
    halo, mask_hbm, outs = ins[: -pieces - 1], ins[-pieces - 1], ins[-pieces:]
    frames, _, ny = out_ref.shape[:3]
    nx = feat.shape[1]
    inside = slice(edge, nx + edge)
    groups = []
    for f in range(frames):
        moves = [
            (feat.at[first + f], ext.at[f, inside, 1 : ny + 1]),
            (halo[0].at[f], ext.at[f, inside, 0:1]),
            (halo[1].at[f], ext.at[f, inside, ny + 1 : ny + 2]),
        ]
        if f == 0:
            moves += [
                (mask_hbm.at[x * ny : (x + 1) * ny], mask_ref.at[i * ny : (i + 1) * ny])
                for i, x in enumerate(xs)
            ]
        if edge:
            xlo, xhi, clo, chi = (ref.at[f] for ref in halo[2:])
            moves += [
                (xlo, ext.at[f, 0:1, 1 : ny + 1]),
                (xhi, ext.at[f, nx + 1 : nx + 2, 1 : ny + 1]),
                (clo.at[0:1], ext.at[f, 0:1, 0:1]),
                (clo.at[1:2], ext.at[f, nx + 1 : nx + 2, 0:1]),
                (chi.at[0:1], ext.at[f, 0:1, ny + 1 : ny + 2]),
                (chi.at[1:2], ext.at[f, nx + 1 : nx + 2, ny + 1 : ny + 2]),
            ]
        groups.append(moves)
    copies, used = [], 0
    for moves in groups:
        copies.append(
            [
                pltpu.make_async_copy(src, dst, sems.at[used + i])
                for i, (src, dst) in enumerate(moves)
            ]
        )
        used += len(moves)
        for copy in copies[-1]:
            copy.start()
    slots = mask_ref.shape[2] // mask_ref.shape[1]
    sent = []
    for f in range(frames):
        for copy in copies[f]:
            copy.wait()
        for i, x in enumerate(xs):
            for y in range(ny):
                places = []
                for k in range(slots):
                    code = codes[(x * ny + y) * slots + k]
                    places.append(
                        (x - 1 + edge + lax.div(code, 3), y + lax.rem(code, 3))
                    )
                source = jnp.concatenate([ext[f, sx, sy] for sx, sy in places], axis=0)
                summed = jnp.dot(
                    mask_ref[i * ny + y], source, preferred_element_type=F32
                )
                out_ref[f, i, y] = (0.18 * summed).astype(BF16)
        piece = len(xs) // pieces
        for n, out in enumerate(outs):
            rows = slice(n * piece, (n + 1) * piece)
            copy = pltpu.make_async_copy(
                out_ref.at[f, rows], out.at[f], sems.at[used + f * pieces + n]
            )
            copy.start()
            sent.append(copy)
    for copy in sent:
        copy.wait()


def aggregate(first, xs, codes, features, halo, mask, pieces=1):
    _, nx, ny, lipids, width = features.shape
    frames = 2
    slots = mask.shape[2] // lipids
    edge = 1 if len(halo) > 2 else 0
    anywhere = pl.BlockSpec(memory_space=pl.ANY)
    flops = 2 * frames * len(xs) * ny * lipids * mask.shape[2] * width
    out_shape = (frames, len(xs), ny, lipids, width)
    out = pl.pallas_call(
        functools.partial(agg_kernel, first, xs, edge, pieces),
        in_specs=[pl.BlockSpec(memory_space=pltpu.SMEM)] + [anywhere] * (len(halo) + 2),
        out_specs=[anywhere] * pieces,
        out_shape=[
            jax.ShapeDtypeStruct(
                (frames, len(xs) // pieces, ny, lipids, width), BF16
            )
        ]
        * pieces,
        scratch_shapes=[
            pltpu.VMEM((frames, nx + 2 * edge, ny + 2, lipids, width), BF16),
            pltpu.VMEM((len(xs) * ny, lipids, slots * lipids), BF16),
            pltpu.VMEM(out_shape, BF16),
            pltpu.SemaphoreType.DMA((frames * (12 + len(xs)),)),
        ],
        compiler_params=pltpu.CompilerParams(vmem_limit_bytes=VMEM),
        cost_estimate=pl.CostEstimate(
            flops=flops, bytes_accessed=8 << 20, transcendentals=0
        ),
        name="aggregate",
    )(codes, features, *halo, mask)
    return [piece.reshape(frames, -1, width) for piece in out]


def mix_kernel(half, places, *refs):
    p_hbm, q_hbm, feat_hbm, cot_hbm, v_hbm, *given = refs[:-9]
    up_hbm, g_ref, p_ref, q_ref, feat_ref, cot_ref, v_ref, up_ref, sems = refs[-9:]
    rows, count = MIX_ROWS, len(places)
    pair = slice(2 * half, 2 * half + 2)
    loads = [[pltpu.make_async_copy(v_hbm, v_ref, sems.at[0])]]
    for c, place in enumerate(places):
        here, there = slice(c * rows, (c + 1) * rows), slice(place, place + rows)
        loads += [
            [
                pltpu.make_async_copy(src, dst.at[:, here], sems.at[1 + 4 * c + i])
                for i, (src, dst) in enumerate(
                    (
                        (q_hbm.at[:, here], q_ref),
                        (p_hbm.at[:, here], p_ref),
                        (feat_hbm.at[pair, there], feat_ref),
                        (cot_hbm.at[pair, there], cot_ref),
                    )
                )
            ]
        ]
    stores = [
        pltpu.make_async_copy(
            up_ref.at[:, c * rows : (c + 1) * rows],
            up_hbm.at[pair, place : place + rows],
            sems.at[1 + 4 * count + c],
        )
        for c, place in enumerate(places)
    ]
    for copy in sum(loads, []):
        copy.start()
    loads[0][0].wait()
    g_ref[...] = given[0][...] if given else jnp.zeros_like(g_ref)
    for c in range(count):
        for copy in loads[c + 1]:
            copy.wait()
        here = slice(c * rows, (c + 1) * rows)
        before = [p_ref[0, here], p_ref[1, here], q_ref[0, here], q_ref[1, here]]
        lefts, grads = [], []
        for f in range(2):
            left = jnp.concatenate([before[f + 2], before[f + 1], before[f]], axis=1)
            mixed = jnp.dot(left, v_ref[...], preferred_element_type=F32)
            s = 0.5 * jnp.tanh(0.5 * mixed) + 0.5
            silu = mixed * s
            up_ref[f, here] = (feat_ref[f, here].astype(F32) + silu).astype(BF16)
            grad = cot_ref[f, here].astype(F32) * (s + silu * (1.0 - s))
            lefts.append(left)
            grads.append(grad.astype(BF16))
        stores[c].start()
        g_ref[...] += lax.dot_general(
            jnp.concatenate(lefts, axis=0),
            jnp.concatenate(grads, axis=0),
            (((0,), (0,)), ((), ())),
            preferred_element_type=F32,
        )
    for copy in stores:
        copy.wait()


def mix(half, places, prev, now, features, cotangent, v, given=(), vmem=None):
    frames, count, width = now.shape
    anywhere = pl.BlockSpec(memory_space=pl.ANY)
    block = pltpu.VMEM(now.shape, BF16)
    return pl.pallas_call(
        functools.partial(mix_kernel, half, places),
        in_specs=[anywhere] * 5 + ([whole_vmem(), anywhere] if given else []),
        out_specs=[anywhere, whole_vmem()],
        out_shape=[
            jax.ShapeDtypeStruct(features.shape, BF16),
            jax.ShapeDtypeStruct(v.shape, F32),
        ],
        scratch_shapes=[block] * 4
        + [
            pltpu.VMEM(v.shape, BF16),
            block,
            pltpu.SemaphoreType.DMA((1 + 5 * len(places),)),
        ],
        input_output_aliases={6: 0} if given else {},
        compiler_params=pltpu.CompilerParams(vmem_limit_bytes=vmem or VMEM),
        cost_estimate=pl.CostEstimate(flops=1, bytes_accessed=1, transcendentals=0),
        name="mix",
    )(prev, now, features, cotangent, v, *given)


def finish_kernel(scale, g_ref, ws_ref, wt_ref, space_ref, time_ref):
    width = ws_ref.shape[0]
    space = jnp.zeros((width, width), F32)
    for j in range(wt_ref.shape[0]):
        g = g_ref[j * width : (j + 1) * width, :]
        high = g.astype(BF16)
        low = (g - high.astype(F32)).astype(BF16)
        time = 0.0
        for part in (low, high):
            time = time + lax.dot_general(
                ws_ref[...], part, (((0,), (0,)), ((), ())), preferred_element_type=F32
            )
            space = space + lax.dot_general(
                part, wt_ref[j], (((1,), (1,)), ((), ())), preferred_element_type=F32
            )
        time_ref[j] = time * scale
    space_ref[...] = space * scale


def finish(scale, total, w_space, w_time):
    return pl.pallas_call(
        functools.partial(finish_kernel, scale),
        in_specs=[whole_vmem()] * 3,
        out_specs=[whole_vmem()] * 2,
        out_shape=[
            jax.ShapeDtypeStruct(w_space.shape, F32),
            jax.ShapeDtypeStruct(w_time.shape, F32),
        ],
        compiler_params=pltpu.CompilerParams(vmem_limit_bytes=20 << 20),
        name="finish",
    )(total, w_space, w_time)


def all_sum(total):
    rows, width = total.shape
    half, block = rows // 2, 8
    count = lax.axis_size(REST)
    me = lax.axis_index("core")
    keep = lax.dynamic_slice_in_dim(total, me * half, half, 0)
    give = lax.dynamic_slice_in_dim(total, (1 - me) * half, half, 0)
    mine = keep + lax.ppermute(give, "core", ring(2, 1))
    mine = jnp.pad(mine, ((0, count * block - half), (0, 0)))
    mine = lax.all_to_all(mine.reshape(count, block, width), REST, 0, 0, tiled=True)
    spread = jnp.broadcast_to(mine.sum(axis=0)[None], (count, block, width))
    back = lax.all_to_all(spread, REST, 0, 0, tiled=True)
    back = back.reshape(count * block, width)[:half]
    other = lax.ppermute(back, "core", ring(2, 1))
    return jnp.where(
        me == 0, jnp.concatenate([back, other]), jnp.concatenate([other, back])
    )


def shards(features, neighbours, adjacency, w_space, w_time, cotangent):
    frames, nx, ny, lipids, width = features.shape
    count = nx * ny * lipids
    codes = neighbours.reshape(-1)
    up, down = ring(4, 1), ring(4, -1)
    onward = [(i, i + 1) for i in range(7)]
    inner, outer = tuple(range(1, nx - 1)), (0, nx - 1)

    every = slice(None)
    low, high = slice(0, 1), slice(ny - 1, ny)

    def exchange(axis, high_edge, low_edge):
        return lax.ppermute(high_edge, axis, up), lax.ppermute(low_edge, axis, down)

    def edges(first, source):
        pair = slice(first, first + 2)
        x_edge, y_edge = (2, 1, ny, lipids, width), (2, nx, 1, lipids, width)
        return pack(
            [source],
            [x_edge, x_edge, y_edge, y_edge],
            [
                (0, (pair, slice(nx - 1, nx)), 0, ()),
                (0, (pair, low), 1, ()),
                (0, (pair, every, high), 2, ()),
                (0, (pair, every, low), 3, ()),
            ],
        )

    def corners(x_halo):
        corner = (2, 2, 1, lipids, width)
        ends = pack(
            x_halo,
            [corner, corner],
            [
                (i, (every, every, side), o, (every, slice(i, i + 1)))
                for i in range(2)
                for o, side in enumerate((high, low))
            ],
        )
        return exchange("gy", *ends)

    edges_b = edges(2, features)
    x_b = exchange(GX, *edges_b[:2])
    y_b = exchange("gy", *edges_b[2:])
    mask, v = prep(adjacency.reshape(nx * ny, -1, lipids, lipids), w_space, w_time)
    later, _, _ = lax.optimization_barrier((features, edges_b, mask))
    edges_a = edges(0, later)
    x_a = exchange(GX, *edges_a[:2])
    y_a = exchange("gy", *edges_a[2:])
    c_b = corners(x_b)
    (inner_b,) = aggregate(2, inner, codes, features, y_b, mask)
    prev_inner = lax.ppermute(inner_b, "ta", onward)
    c_b, _, _, _ = lax.optimization_barrier((c_b, inner_b, x_a, y_a))
    outer_b = aggregate(2, outer, codes, features, (*y_b, *x_b, *c_b), mask, 2)
    prev_first = lax.ppermute(outer_b[0], "ta", onward)
    prev_last = lax.ppermute(outer_b[1], "ta", onward)
    x_a, y_a, mask_a, _ = lax.optimization_barrier((x_a, y_a, mask, outer_b))
    c_a = corners(x_a)
    (inner_a,) = aggregate(0, inner, codes, features, y_a, mask_a)
    outer_a = aggregate(0, outer, codes, features, (*y_a, *x_a, *c_a), mask_a, 2)
    feat = features.reshape(frames, count, width)
    cot = cotangent.reshape(frames, count, width)
    a_row = ny * lipids
    groups = [inner, outer[:1], outer[1:]]
    chunks = [
        [x * a_row + r for x in xs for r in range(0, a_row, MIX_ROWS)] for xs in groups
    ]
    now_b, now_a = (inner_b, *outer_b), (inner_a, *outer_a)
    state = ()
    for chunk, prev, now in zip(chunks, now_a, now_b):
        updated, total = mix(1, chunk, prev, now, feat, cot, v, state)
        state = (total, updated)
    for chunk, prev, now in zip(chunks, (prev_inner, prev_first, prev_last), now_a):
        updated, total = mix(0, chunk, prev, now, feat, cot, v, state)
        state = (total, updated)
    total = all_sum(total)
    scale = 1.0 / math.sqrt(frames * count * lax.axis_size(EVERY))
    grad_space, grad_time = finish(scale, total, w_space, w_time)
    return updated.reshape(features.shape), grad_space, grad_time


def solution(mesh):
    gx, gy, ta = (mesh.shape[a] for a in ("gx", "gy", "ta"))
    fine = Mesh(
        np.asarray(mesh.devices).reshape(2, gx // 2, gy, ta), ("yh", "core", "gy", "ta")
    )
    in_specs = (
        P("ta", GX, "gy", None, None),
        P(GX, "gy", None),
        P(GX, "gy", None, None, None),
        P(),
        P(),
        P("ta", GX, "gy", None, None),
    )
    out_specs = (P("ta", GX, "gy", None, None), P(), P())
    return jax.shard_map(shards, mesh=fine, in_specs=in_specs, out_specs=out_specs, check_vma=False)
```

```python
import functools
import math

import jax
import jax.numpy as jnp
import numpy as np
from jax import lax
from jax.experimental import pallas as pl
from jax.experimental.pallas import tpu as pltpu
from jax.sharding import Mesh
from jax.sharding import PartitionSpec as P

BF16 = jnp.bfloat16
F32 = jnp.float32
GX = ("yh", "core")
MIX_ROWS = 256
VMEM = 65300 << 10
EVERY = ("yh", "core", "gy", "ta")
REST = ("yh", "gy", "ta")


def ring(count, step):
    return [(i, (i + step) % count) for i in range(count)]


def whole_vmem():
    return pl.BlockSpec(memory_space=pltpu.VMEM)


def prep_kernel(adj_ref, ws_ref, wt_ref, mask_ref, v_ref):
    slots, lipids = adj_ref.shape[1], adj_ref.shape[2]
    width = ws_ref.shape[1]
    for t in range(adj_ref.shape[0]):
        for k in range(slots):
            mask_ref[t, :, k * lipids : (k + 1) * lipids] = (
                adj_ref[t, k].astype(F32).astype(BF16)
            )

    @pl.when(pl.program_id(0) == 0)
    def _():
        for j in range(wt_ref.shape[0]):
            v_ref[j * width : (j + 1) * width, :] = jnp.dot(
                ws_ref[...], wt_ref[j], preferred_element_type=F32
            ).astype(BF16)


def prep(adjacency, w_space, w_time):
    tiles, slots, lipids, _ = adjacency.shape
    taps, width, _ = w_time.shape
    return pl.pallas_call(
        prep_kernel,
        grid=(tiles // 4,),
        in_specs=[
            pl.BlockSpec((4, slots, lipids, lipids), lambda i: (i, 0, 0, 0)),
            pl.BlockSpec((width, width), lambda i: (0, 0)),
            pl.BlockSpec((taps, width, width), lambda i: (0, 0, 0)),
        ],
        out_specs=[
            pl.BlockSpec((4, lipids, slots * lipids), lambda i: (i, 0, 0)),
            pl.BlockSpec((taps * width, width), lambda i: (0, 0)),
        ],
        out_shape=[
            jax.ShapeDtypeStruct((tiles, lipids, slots * lipids), BF16),
            jax.ShapeDtypeStruct((taps * width, width), BF16),
        ],
        compiler_params=pltpu.CompilerParams(vmem_limit_bytes=VMEM),
        cost_estimate=pl.CostEstimate(
            flops=2 * taps * width**3, bytes_accessed=8 << 20, transcendentals=0
        ),
        name="prep",
    )(adjacency, w_space, w_time)


def pack_kernel(moves, count, *refs):
    *arrays, sems = refs
    copies = [
        pltpu.make_async_copy(arrays[i].at[src], arrays[count + o].at[dst], sems.at[n])
        for n, (i, src, o, dst) in enumerate(moves)
    ]
    for copy in copies:
        copy.start()
    for copy in copies:
        copy.wait()


def pack(arrays, shapes, moves):
    anywhere = pl.BlockSpec(memory_space=pl.ANY)
    return pl.pallas_call(
        functools.partial(pack_kernel, moves, len(arrays)),
        in_specs=[anywhere] * len(arrays),
        out_specs=[whole_vmem()] * len(shapes),
        out_shape=[jax.ShapeDtypeStruct(shape, BF16) for shape in shapes],
        scratch_shapes=[pltpu.SemaphoreType.DMA((len(moves),))],
        compiler_params=pltpu.CompilerParams(vmem_limit_bytes=VMEM),
        cost_estimate=pl.CostEstimate(flops=0, bytes_accessed=6 << 20, transcendentals=0),
        name="pack",
    )(*arrays)


def agg_kernel(first, xs, edge, pieces, codes, feat, *rest):
    *ins, ext, mask_ref, out_ref, sems = rest
    halo, mask_hbm, outs = ins[: -pieces - 1], ins[-pieces - 1], ins[-pieces:]
    frames, _, ny = out_ref.shape[:3]
    nx = feat.shape[1]
    inside = slice(edge, nx + edge)
    groups = []
    for f in range(frames):
        moves = [
            (feat.at[first + f], ext.at[f, inside, 1 : ny + 1]),
            (halo[0].at[f], ext.at[f, inside, 0:1]),
            (halo[1].at[f], ext.at[f, inside, ny + 1 : ny + 2]),
        ]
        if f == 0:
            moves += [
                (mask_hbm.at[x * ny : (x + 1) * ny], mask_ref.at[i * ny : (i + 1) * ny])
                for i, x in enumerate(xs)
            ]
        if edge:
            xlo, xhi = (ref.at[first + f] for ref in halo[2:4])
            clo, chi = (ref.at[f] for ref in halo[4:])
            moves += [
                (xlo, ext.at[f, 0:1, 1 : ny + 1]),
                (xhi, ext.at[f, nx + 1 : nx + 2, 1 : ny + 1]),
                (clo.at[0:1], ext.at[f, 0:1, 0:1]),
                (clo.at[1:2], ext.at[f, nx + 1 : nx + 2, 0:1]),
                (chi.at[0:1], ext.at[f, 0:1, ny + 1 : ny + 2]),
                (chi.at[1:2], ext.at[f, nx + 1 : nx + 2, ny + 1 : ny + 2]),
            ]
        groups.append(moves)
    copies, used = [], 0
    for moves in groups:
        copies.append(
            [
                pltpu.make_async_copy(src, dst, sems.at[used + i])
                for i, (src, dst) in enumerate(moves)
            ]
        )
        used += len(moves)
        for copy in copies[-1]:
            copy.start()
    slots = mask_ref.shape[2] // mask_ref.shape[1]
    sent = []
    for f in range(frames):
        for copy in copies[f]:
            copy.wait()
        for i, x in enumerate(xs):
            for y in range(ny):
                places = []
                for k in range(slots):
                    code = codes[(x * ny + y) * slots + k]
                    places.append(
                        (x - 1 + edge + lax.div(code, 3), y + lax.rem(code, 3))
                    )
                source = jnp.concatenate([ext[f, sx, sy] for sx, sy in places], axis=0)
                summed = jnp.dot(
                    mask_ref[i * ny + y], source, preferred_element_type=F32
                )
                out_ref[f, i, y] = (0.18 * summed).astype(BF16)
        piece = len(xs) // pieces
        for n, out in enumerate(outs):
            rows = slice(n * piece, (n + 1) * piece)
            copy = pltpu.make_async_copy(
                out_ref.at[f, rows], out.at[f], sems.at[used + f * pieces + n]
            )
            copy.start()
            sent.append(copy)
    for copy in sent:
        copy.wait()


def aggregate(first, xs, codes, features, halo, mask, pieces=1):
    _, nx, ny, lipids, width = features.shape
    frames = 2
    slots = mask.shape[2] // lipids
    edge = 1 if len(halo) > 2 else 0
    anywhere = pl.BlockSpec(memory_space=pl.ANY)
    flops = 2 * frames * len(xs) * ny * lipids * mask.shape[2] * width
    out_shape = (frames, len(xs), ny, lipids, width)
    out = pl.pallas_call(
        functools.partial(agg_kernel, first, xs, edge, pieces),
        in_specs=[pl.BlockSpec(memory_space=pltpu.SMEM)] + [anywhere] * (len(halo) + 2),
        out_specs=[anywhere] * pieces,
        out_shape=[
            jax.ShapeDtypeStruct(
                (frames, len(xs) // pieces, ny, lipids, width), BF16
            )
        ]
        * pieces,
        scratch_shapes=[
            pltpu.VMEM((frames, nx + 2 * edge, ny + 2, lipids, width), BF16),
            pltpu.VMEM((len(xs) * ny, lipids, slots * lipids), BF16),
            pltpu.VMEM(out_shape, BF16),
            pltpu.SemaphoreType.DMA((frames * (12 + len(xs)),)),
        ],
        compiler_params=pltpu.CompilerParams(vmem_limit_bytes=VMEM),
        cost_estimate=pl.CostEstimate(
            flops=flops, bytes_accessed=8 << 20, transcendentals=0
        ),
        name="aggregate",
    )(codes, features, *halo, mask)
    return [piece.reshape(frames, -1, width) for piece in out]


def mix_kernel(half, chunks, sizes, final, *refs):
    n_prev, n_now = sizes
    prevs, nows = refs[:n_prev], refs[n_prev : n_prev + n_now]
    feat_hbm, cot_hbm, v_hbm, *refs = refs[n_prev + n_now :]
    *refs, p_ref, q_ref, feat_ref, cot_ref, v_ref, up_ref, g_ref, given_ref, sems = refs
    given = refs[0] if half == 0 else None
    up_hbm, outs = refs[-2 - final], refs[-1 - final :]
    rows, count = MIX_ROWS, len(chunks)
    pair = slice(2 * half, 2 * half + 2)
    first = pltpu.make_async_copy(v_hbm, v_ref, sems.at[0])
    last = pltpu.make_async_copy(given, given_ref, sems.at[1]) if given is not None else None
    loads, stores = [], []
    for c, (p, p_row, q, q_row, place) in enumerate(chunks):
        here, there = slice(c * rows, (c + 1) * rows), slice(place, place + rows)
        moves = (
            (nows[q].at[:, q_row : q_row + rows], q_ref),
            (prevs[p].at[:, p_row : p_row + rows], p_ref),
            (feat_hbm.at[pair, there], feat_ref),
            (cot_hbm.at[pair, there], cot_ref),
        )
        loads.append(
            [
                pltpu.make_async_copy(src, dst.at[:, here], sems.at[2 + 5 * c + i])
                for i, (src, dst) in enumerate(moves)
            ]
        )
        stores.append(
            pltpu.make_async_copy(
                up_ref.at[:, here], up_hbm.at[pair, there], sems.at[2 + 5 * c + 4]
            )
        )
    first.start()
    for copy in sum(loads, []):
        copy.start()
    if last is not None:
        last.start()
    first.wait()
    for c in range(count):
        for copy in loads[c]:
            copy.wait()
        here = slice(c * rows, (c + 1) * rows)
        before = [p_ref[0, here], p_ref[1, here], q_ref[0, here], q_ref[1, here]]
        lefts, grads = [], []
        for f in range(2):
            left = jnp.concatenate([before[f + 2], before[f + 1], before[f]], axis=1)
            mixed = jnp.dot(left, v_ref[...], preferred_element_type=F32)
            s = 0.5 * jnp.tanh(0.5 * mixed) + 0.5
            silu = mixed * s
            up_ref[f, here] = (feat_ref[f, here].astype(F32) + silu).astype(BF16)
            grad = cot_ref[f, here].astype(F32) * (s + silu * (1.0 - s))
            lefts.append(left)
            grads.append(grad.astype(BF16))
        stores[c].start()
        terms = lax.dot_general(
            jnp.concatenate(lefts, axis=0),
            jnp.concatenate(grads, axis=0),
            (((0,), (0,)), ((), ())),
            preferred_element_type=F32,
        )
        g_ref[...] = terms if c == 0 else g_ref[...] + terms
    if last is not None:
        last.wait()
    if final:
        me = refs[1][0]
        share = g_ref.shape[0] // 2
        low, high = slice(0, share), slice(share, 2 * share)
        for core, (mine, theirs) in enumerate(((low, high), (high, low))):

            @pl.when(me == core)
            def _(mine=mine, theirs=theirs):
                outs[0][...] = g_ref[mine] + given_ref[mine]
                outs[1][...] = g_ref[theirs] + given_ref[theirs]

    else:
        outs[0][...] = g_ref[...] + given_ref[...] if last is not None else g_ref[...]
    for copy in stores:
        copy.wait()


def mix(half, chunks, prevs, nows, features, cotangent, v, given=None, me=None):
    frames, width = 2, v.shape[1]
    anywhere = pl.BlockSpec(memory_space=pl.ANY)
    block = pltpu.VMEM((frames, len(chunks) * MIX_ROWS, width), BF16)
    sums = jax.ShapeDtypeStruct(v.shape, F32)
    share = jax.ShapeDtypeStruct((v.shape[0] // 2, width), F32)
    arrays = [*prevs, *nows, features, cotangent, v]
    specs = [anywhere] * len(arrays)
    aliases = {}
    if given is not None:
        final = 1 if me is not None else 0
        total, updated = given
        core = me if final else jnp.zeros((1,), jnp.int32)
        arrays += [total, core, updated]
        aliases = {len(arrays) - 1: 0}
        specs += [anywhere, pl.BlockSpec(memory_space=pltpu.SMEM), anywhere]
    else:
        final = 0
    return pl.pallas_call(
        functools.partial(mix_kernel, half, chunks, (len(prevs), len(nows)), final),
        in_specs=specs,
        out_specs=[anywhere] + [whole_vmem()] * (1 + final),
        out_shape=[jax.ShapeDtypeStruct(features.shape, BF16)]
        + ([share, share] if final else [sums]),
        scratch_shapes=[block] * 4
        + [
            pltpu.VMEM(v.shape, BF16),
            block,
            pltpu.VMEM(v.shape, F32),
            pltpu.VMEM(v.shape, F32),
            pltpu.SemaphoreType.DMA((2 + 5 * len(chunks),)),
        ],
        input_output_aliases=aliases,
        compiler_params=pltpu.CompilerParams(vmem_limit_bytes=VMEM),
        cost_estimate=pl.CostEstimate(flops=1, bytes_accessed=1, transcendentals=0),
        name="mix",
    )(*arrays)


def finish_kernel(scale, g_ref, ws_ref, wt_ref, space_ref, time_ref):
    width = ws_ref.shape[0]
    space = jnp.zeros((width, width), F32)
    for j in range(wt_ref.shape[0]):
        g = g_ref[j * width : (j + 1) * width, :]
        high = g.astype(BF16)
        low = (g - high.astype(F32)).astype(BF16)
        time = 0.0
        for part in (low, high):
            time = time + lax.dot_general(
                ws_ref[...], part, (((0,), (0,)), ((), ())), preferred_element_type=F32
            )
            space = space + lax.dot_general(
                part, wt_ref[j], (((1,), (1,)), ((), ())), preferred_element_type=F32
            )
        time_ref[j] = time * scale
    space_ref[...] = space * scale


def finish(scale, total, w_space, w_time):
    return pl.pallas_call(
        functools.partial(finish_kernel, scale),
        in_specs=[whole_vmem()] * 3,
        out_specs=[whole_vmem()] * 2,
        out_shape=[
            jax.ShapeDtypeStruct(w_space.shape, F32),
            jax.ShapeDtypeStruct(w_time.shape, F32),
        ],
        compiler_params=pltpu.CompilerParams(vmem_limit_bytes=20 << 20),
        name="finish",
    )(total, w_space, w_time)


def all_sum(keep, give):
    half, width = keep.shape
    block, count = 8, lax.axis_size(REST)
    mine = keep + lax.ppermute(give, "core", ring(2, 1))
    mine = jnp.pad(mine, ((0, count * block - half), (0, 0)))
    mine = lax.all_to_all(mine.reshape(count, block, width), REST, 0, 0, tiled=True)
    spread = jnp.broadcast_to(mine.sum(axis=0)[None], (count, block, width))
    back = lax.all_to_all(spread, REST, 0, 0, tiled=True)
    back = back.reshape(count * block, width)[:half]
    other = lax.ppermute(back, "core", ring(2, 1))
    first = lax.axis_index("core") == 0
    return jnp.where(
        first, jnp.concatenate([back, other]), jnp.concatenate([other, back])
    )


def shards(features, neighbours, adjacency, w_space, w_time, cotangent):
    frames, nx, ny, lipids, width = features.shape
    count = nx * ny * lipids
    codes = neighbours.reshape(-1)
    up, down = ring(4, 1), ring(4, -1)
    onward = [(i, i + 1) for i in range(7)]
    inner, outer = tuple(range(1, nx - 1)), (0, nx - 1)

    every = slice(None)
    low, high = slice(0, 1), slice(ny - 1, ny)

    def exchange(axis, high_edge, low_edge):
        return lax.ppermute(high_edge, axis, up), lax.ppermute(low_edge, axis, down)

    def x_edges(source):
        edge = (frames, 1, ny, lipids, width)
        moves = [(0, (every, slice(nx - 1, nx)), 0, ()), (0, (every, low), 1, ())]
        return pack([source], [edge, edge], moves)

    def y_edges(first, source):
        edge = (2, nx, 1, lipids, width)
        pair = slice(first, first + 2)
        moves = [(0, (pair, every, side), o, ()) for o, side in enumerate((high, low))]
        return pack([source], [edge, edge], moves)

    def corners(first, x_halo):
        corner = (2, 2, 1, lipids, width)
        pair = slice(first, first + 2)
        ends = pack(
            x_halo,
            [corner, corner],
            [
                (i, (pair, every, side), o, (every, slice(i, i + 1)))
                for i in range(2)
                for o, side in enumerate((high, low))
            ],
        )
        return exchange("gy", *ends)

    edges_b = y_edges(2, features)
    y_b = exchange("gy", *edges_b)
    later, _ = lax.optimization_barrier((features, edges_b))
    edges_x = x_edges(later)
    x_halo = exchange(GX, *edges_x)
    later, _ = lax.optimization_barrier((features, edges_x))
    edges_a = y_edges(0, later)
    y_a = exchange("gy", *edges_a)
    contacts = adjacency.reshape(nx * ny, -1, lipids, lipids)
    contacts, _ = lax.optimization_barrier((contacts, edges_x))
    mask, v = prep(contacts, w_space, w_time)
    (inner_b,) = aggregate(2, inner, codes, features, y_b, mask)
    x_halo, y_a, sent = lax.optimization_barrier((x_halo, y_a, inner_b))
    prev_inner = lax.ppermute(sent, "ta", onward)
    c_b = corners(2, x_halo)
    c_a = corners(0, x_halo)
    outer_b = aggregate(2, outer, codes, features, (*y_b, *x_halo, *c_b), mask, 2)
    c_a, sent = lax.optimization_barrier((c_a, outer_b))
    prev_first = lax.ppermute(sent[0], "ta", onward)
    prev_last = lax.ppermute(sent[1], "ta", onward)
    every_x = tuple(range(nx))
    (agg_a,) = aggregate(0, every_x, codes, features, (*y_a, *x_halo, *c_a), mask)
    feat = features.reshape(frames, count, width)
    cot = cotangent.reshape(frames, count, width)
    a_row = ny * lipids
    end = count - a_row
    updated, total = mix(
        1,
        [(0, r, 0, r - a_row, r) for r in range(a_row, end, MIX_ROWS)]
        + [(0, r, 1, r, r) for r in range(0, a_row, MIX_ROWS)]
        + [(0, r, 2, r - end, r) for r in range(end, count, MIX_ROWS)],
        [agg_a],
        [inner_b, *outer_b],
        feat,
        cot,
        v,
    )
    updated, total = mix(
        0,
        [(0, r - a_row, 0, r, r) for r in range(a_row, end, MIX_ROWS)]
        + [(1, r, 0, r, r) for r in range(0, a_row, MIX_ROWS)],
        [prev_inner, prev_first],
        [agg_a],
        feat,
        cot,
        v,
        (total, updated),
    )
    me = lax.axis_index("core").reshape(1)
    updated, keep, give = mix(
        0,
        [(0, r - end, 0, r, r) for r in range(end, count, MIX_ROWS)],
        [prev_last],
        [agg_a],
        feat,
        cot,
        v,
        (total, updated),
        me,
    )
    total = all_sum(keep, give)
    scale = 1.0 / math.sqrt(frames * count * lax.axis_size(EVERY))
    grad_space, grad_time = finish(scale, total, w_space, w_time)
    return updated.reshape(features.shape), grad_space, grad_time


def solution(mesh):
    gx, gy, ta = (mesh.shape[a] for a in ("gx", "gy", "ta"))
    fine = Mesh(
        np.asarray(mesh.devices).reshape(2, gx // 2, gy, ta), ("yh", "core", "gy", "ta")
    )
    in_specs = (
        P("ta", GX, "gy", None, None),
        P(GX, "gy", None),
        P(GX, "gy", None, None, None),
        P(),
        P(),
        P("ta", GX, "gy", None, None),
    )
    out_specs = (P("ta", GX, "gy", None, None), P(), P())
    return jax.shard_map(shards, mesh=fine, in_specs=in_specs, out_specs=out_specs, check_vma=False)
```

```python
import functools
import math

import jax
import jax.numpy as jnp
import numpy as np
from jax import lax
from jax.experimental import pallas as pl
from jax.experimental.pallas import tpu as pltpu
from jax.sharding import Mesh
from jax.sharding import PartitionSpec as P

BF16 = jnp.bfloat16
F32 = jnp.float32
GX = ("yh", "core")
MIX_ROWS = 256
VMEM = 65300 << 10
EVERY = ("yh", "core", "gy", "ta")
REST = ("yh", "gy", "ta")


def ring(count, step):
    return [(i, (i + step) % count) for i in range(count)]


def whole_vmem():
    return pl.BlockSpec(memory_space=pltpu.VMEM)


def prep_kernel(adj_ref, ws_ref, wt_ref, mask_ref, v_ref):
    slots, lipids = adj_ref.shape[1], adj_ref.shape[2]
    width = ws_ref.shape[1]
    for t in range(adj_ref.shape[0]):
        for k in range(slots):
            mask_ref[t, :, k * lipids : (k + 1) * lipids] = (
                adj_ref[t, k].astype(F32).astype(BF16)
            )

    @pl.when(pl.program_id(0) == 0)
    def _():
        for j in range(wt_ref.shape[0]):
            v_ref[j * width : (j + 1) * width, :] = jnp.dot(
                ws_ref[...], wt_ref[j], preferred_element_type=F32
            ).astype(BF16)


def prep(adjacency, w_space, w_time):
    tiles, slots, lipids, _ = adjacency.shape
    taps, width, _ = w_time.shape
    return pl.pallas_call(
        prep_kernel,
        grid=(tiles // 4,),
        in_specs=[
            pl.BlockSpec((4, slots, lipids, lipids), lambda i: (i, 0, 0, 0)),
            pl.BlockSpec((width, width), lambda i: (0, 0)),
            pl.BlockSpec((taps, width, width), lambda i: (0, 0, 0)),
        ],
        out_specs=[
            pl.BlockSpec((4, lipids, slots * lipids), lambda i: (i, 0, 0)),
            pl.BlockSpec((taps * width, width), lambda i: (0, 0)),
        ],
        out_shape=[
            jax.ShapeDtypeStruct((tiles, lipids, slots * lipids), BF16),
            jax.ShapeDtypeStruct((taps * width, width), BF16),
        ],
        compiler_params=pltpu.CompilerParams(vmem_limit_bytes=VMEM),
        cost_estimate=pl.CostEstimate(
            flops=2 * taps * width**3, bytes_accessed=8 << 20, transcendentals=0
        ),
        name="prep",
    )(adjacency, w_space, w_time)


def pack_kernel(moves, count, *refs):
    *arrays, sems = refs
    copies = [
        pltpu.make_async_copy(arrays[i].at[src], arrays[count + o].at[dst], sems.at[n])
        for n, (i, src, o, dst) in enumerate(moves)
    ]
    for copy in copies:
        copy.start()
    for copy in copies:
        copy.wait()


def pack(arrays, shapes, moves):
    anywhere = pl.BlockSpec(memory_space=pl.ANY)
    return pl.pallas_call(
        functools.partial(pack_kernel, moves, len(arrays)),
        in_specs=[anywhere] * len(arrays),
        out_specs=[whole_vmem()] * len(shapes),
        out_shape=[jax.ShapeDtypeStruct(shape, BF16) for shape in shapes],
        scratch_shapes=[pltpu.SemaphoreType.DMA((len(moves),))],
        compiler_params=pltpu.CompilerParams(vmem_limit_bytes=VMEM),
        cost_estimate=pl.CostEstimate(flops=0, bytes_accessed=6 << 20, transcendentals=0),
        name="pack",
    )(*arrays)


def agg_kernel(first, xs, edge, pieces, codes, feat, *rest):
    *ins, ext, mask_ref, out_ref, sems = rest
    halo, mask_hbm, outs = ins[: -pieces - 1], ins[-pieces - 1], ins[-pieces:]
    frames, _, ny = out_ref.shape[:3]
    nx = feat.shape[1]
    inside = slice(edge, nx + edge)
    groups = []
    for f in range(frames):
        moves = [
            (feat.at[first + f], ext.at[f, inside, 1 : ny + 1]),
            (halo[0].at[f], ext.at[f, inside, 0:1]),
            (halo[1].at[f], ext.at[f, inside, ny + 1 : ny + 2]),
        ]
        if f == 0:
            moves += [
                (mask_hbm.at[x * ny : (x + 1) * ny], mask_ref.at[i * ny : (i + 1) * ny])
                for i, x in enumerate(xs)
            ]
        if edge:
            xlo, xhi = (ref.at[first + f] for ref in halo[2:4])
            clo, chi = (ref.at[f] for ref in halo[4:])
            moves += [
                (xlo, ext.at[f, 0:1, 1 : ny + 1]),
                (xhi, ext.at[f, nx + 1 : nx + 2, 1 : ny + 1]),
                (clo.at[0:1], ext.at[f, 0:1, 0:1]),
                (clo.at[1:2], ext.at[f, nx + 1 : nx + 2, 0:1]),
                (chi.at[0:1], ext.at[f, 0:1, ny + 1 : ny + 2]),
                (chi.at[1:2], ext.at[f, nx + 1 : nx + 2, ny + 1 : ny + 2]),
            ]
        groups.append(moves)
    copies, used = [], 0
    for moves in groups:
        copies.append(
            [
                pltpu.make_async_copy(src, dst, sems.at[used + i])
                for i, (src, dst) in enumerate(moves)
            ]
        )
        used += len(moves)
        for copy in copies[-1]:
            copy.start()
    slots = mask_ref.shape[2] // mask_ref.shape[1]
    sent = []
    for f in range(frames):
        for copy in copies[f]:
            copy.wait()
        for i, x in enumerate(xs):
            for y in range(ny):
                places = []
                for k in range(slots):
                    code = codes[(x * ny + y) * slots + k]
                    places.append(
                        (x - 1 + edge + lax.div(code, 3), y + lax.rem(code, 3))
                    )
                source = jnp.concatenate([ext[f, sx, sy] for sx, sy in places], axis=0)
                summed = jnp.dot(
                    mask_ref[i * ny + y], source, preferred_element_type=F32
                )
                out_ref[f, i, y] = (0.18 * summed).astype(BF16)
        piece = len(xs) // pieces
        for n, out in enumerate(outs):
            rows = slice(n * piece, (n + 1) * piece)
            copy = pltpu.make_async_copy(
                out_ref.at[f, rows], out.at[f], sems.at[used + f * pieces + n]
            )
            copy.start()
            sent.append(copy)
    for copy in sent:
        copy.wait()


def aggregate(first, xs, codes, features, halo, mask, pieces=1):
    _, nx, ny, lipids, width = features.shape
    frames = 2
    slots = mask.shape[2] // lipids
    edge = 1 if len(halo) > 2 else 0
    anywhere = pl.BlockSpec(memory_space=pl.ANY)
    flops = 2 * frames * len(xs) * ny * lipids * mask.shape[2] * width
    out_shape = (frames, len(xs), ny, lipids, width)
    out = pl.pallas_call(
        functools.partial(agg_kernel, first, xs, edge, pieces),
        in_specs=[pl.BlockSpec(memory_space=pltpu.SMEM)] + [anywhere] * (len(halo) + 2),
        out_specs=[anywhere] * pieces,
        out_shape=[
            jax.ShapeDtypeStruct(
                (frames, len(xs) // pieces, ny, lipids, width), BF16
            )
        ]
        * pieces,
        scratch_shapes=[
            pltpu.VMEM((frames, nx + 2 * edge, ny + 2, lipids, width), BF16),
            pltpu.VMEM((len(xs) * ny, lipids, slots * lipids), BF16),
            pltpu.VMEM(out_shape, BF16),
            pltpu.SemaphoreType.DMA((frames * (12 + len(xs)),)),
        ],
        compiler_params=pltpu.CompilerParams(vmem_limit_bytes=VMEM),
        cost_estimate=pl.CostEstimate(
            flops=flops, bytes_accessed=8 << 20, transcendentals=0
        ),
        name="aggregate",
    )(codes, features, *halo, mask)
    return [piece.reshape(frames, -1, width) for piece in out]


def chunk_terms(before, features, cotangents, v_ref):
    lefts, grads, updates = [], [], []
    for f in range(2):
        left = jnp.concatenate([before[f + 2], before[f + 1], before[f]], axis=1)
        mixed = jnp.dot(left, v_ref[...], preferred_element_type=F32)
        s = 0.5 * jnp.tanh(0.5 * mixed) + 0.5
        silu = mixed * s
        updates.append((features[f].astype(F32) + silu).astype(BF16))
        grad = cotangents[f].astype(F32) * (s + silu * (1.0 - s))
        lefts.append(left)
        grads.append(grad.astype(BF16))
    terms = lax.dot_general(
        jnp.concatenate(lefts, axis=0),
        jnp.concatenate(grads, axis=0),
        (((0,), (0,)), ((), ())),
        preferred_element_type=F32,
    )
    return updates, terms


def mix_kernel(half, chunks, sizes, final, *refs):
    n_prev, n_now = sizes
    prevs, nows = refs[:n_prev], refs[n_prev : n_prev + n_now]
    feat_hbm, cot_hbm, v_hbm, *refs = refs[n_prev + n_now :]
    *refs, p_ref, q_ref, feat_ref, cot_ref, v_ref, up_ref, g_ref, given_ref, sems = refs
    given = refs[0] if half == 0 else None
    up_hbm, outs = refs[-2 - final], refs[-1 - final :]
    rows, count = MIX_ROWS, len(chunks)
    pair = slice(2 * half, 2 * half + 2)
    first = pltpu.make_async_copy(v_hbm, v_ref, sems.at[0])
    last = pltpu.make_async_copy(given, given_ref, sems.at[1]) if given is not None else None
    loads, stores = [], []
    for c, (p, p_row, q, q_row, place) in enumerate(chunks):
        here, there = slice(c * rows, (c + 1) * rows), slice(place, place + rows)
        moves = (
            (nows[q].at[:, q_row : q_row + rows], q_ref),
            (prevs[p].at[:, p_row : p_row + rows], p_ref),
            (feat_hbm.at[pair, there], feat_ref),
            (cot_hbm.at[pair, there], cot_ref),
        )
        loads.append(
            [
                pltpu.make_async_copy(src, dst.at[:, here], sems.at[2 + 5 * c + i])
                for i, (src, dst) in enumerate(moves)
            ]
        )
        stores.append(
            pltpu.make_async_copy(
                up_ref.at[:, here], up_hbm.at[pair, there], sems.at[2 + 5 * c + 4]
            )
        )
    first.start()
    for copy in sum(loads, []):
        copy.start()
    if last is not None:
        last.start()
    first.wait()
    for c in range(count):
        for copy in loads[c]:
            copy.wait()
        here = slice(c * rows, (c + 1) * rows)
        before = [p_ref[0, here], p_ref[1, here], q_ref[0, here], q_ref[1, here]]
        updates, terms = chunk_terms(
            before,
            [feat_ref[f, here] for f in range(2)],
            [cot_ref[f, here] for f in range(2)],
            v_ref,
        )
        for f in range(2):
            up_ref[f, here] = updates[f]
        stores[c].start()
        g_ref[...] = terms if c == 0 else g_ref[...] + terms
    if last is not None:
        last.wait()
    if final:
        me = refs[1][0]
        share = g_ref.shape[0] // 2
        low, high = slice(0, share), slice(share, 2 * share)
        for core, (mine, theirs) in enumerate(((low, high), (high, low))):

            @pl.when(me == core)
            def _(mine=mine, theirs=theirs):
                outs[0][...] = g_ref[mine] + given_ref[mine]
                outs[1][...] = g_ref[theirs] + given_ref[theirs]

    else:
        outs[0][...] = g_ref[...] + given_ref[...] if last is not None else g_ref[...]
    for copy in stores:
        copy.wait()


def mix(half, chunks, prevs, nows, features, cotangent, v, given=None, me=None):
    frames, width = 2, v.shape[1]
    anywhere = pl.BlockSpec(memory_space=pl.ANY)
    block = pltpu.VMEM((frames, len(chunks) * MIX_ROWS, width), BF16)
    sums = jax.ShapeDtypeStruct(v.shape, F32)
    share = jax.ShapeDtypeStruct((v.shape[0] // 2, width), F32)
    arrays = [*prevs, *nows, features, cotangent, v]
    specs = [anywhere] * len(arrays)
    aliases = {}
    if given is not None:
        final = 1 if me is not None else 0
        total, updated = given
        core = me if final else jnp.zeros((1,), jnp.int32)
        arrays += [total, core, updated]
        aliases = {len(arrays) - 1: 0}
        specs += [anywhere, pl.BlockSpec(memory_space=pltpu.SMEM), anywhere]
    else:
        final = 0
    return pl.pallas_call(
        functools.partial(mix_kernel, half, chunks, (len(prevs), len(nows)), final),
        in_specs=specs,
        out_specs=[anywhere] + [whole_vmem()] * (1 + final),
        out_shape=[jax.ShapeDtypeStruct(features.shape, BF16)]
        + ([share, share] if final else [sums]),
        scratch_shapes=[block] * 4
        + [
            pltpu.VMEM(v.shape, BF16),
            block,
            pltpu.VMEM(v.shape, F32),
            pltpu.VMEM(v.shape, F32),
            pltpu.SemaphoreType.DMA((2 + 5 * len(chunks),)),
        ],
        input_output_aliases=aliases,
        compiler_params=pltpu.CompilerParams(vmem_limit_bytes=VMEM),
        cost_estimate=pl.CostEstimate(flops=1, bytes_accessed=1, transcendentals=0),
        name="mix",
    )(*arrays)


def middle_kernel(row, codes, feat, *refs):
    ins, scratch = refs[:16], refs[16:]
    halo, mask_hbm, nows = ins[:6], ins[6], ins[7:10]
    prev_hbm, flat_hbm, cot_hbm, v_hbm, agg_hbm, up_hbm = ins[10:]
    g_out, ext, mask_ref, agg_ref, q_ref, p_ref, feat_ref, cot_ref, up_ref, v_ref, sems = scratch
    _, nx, ny, lipids, _ = feat.shape
    count, rows = nx * ny * lipids, MIX_ROWS
    end = count - row
    used = [0]

    def copy(src, dst):
        used[0] += 1
        return pltpu.make_async_copy(src, dst, sems.at[used[0] - 1])

    groups = []
    for f in range(2):
        moves = [
            copy(feat.at[f], ext.at[f, 1 : nx + 1, 1 : ny + 1]),
            copy(halo[0].at[f], ext.at[f, 1 : nx + 1, 0:1]),
            copy(halo[1].at[f], ext.at[f, 1 : nx + 1, ny + 1 : ny + 2]),
            copy(halo[2].at[f], ext.at[f, 0:1, 1 : ny + 1]),
            copy(halo[3].at[f], ext.at[f, nx + 1 : nx + 2, 1 : ny + 1]),
            copy(halo[4].at[f, 0:1], ext.at[f, 0:1, 0:1]),
            copy(halo[4].at[f, 1:2], ext.at[f, nx + 1 : nx + 2, 0:1]),
            copy(halo[5].at[f, 0:1], ext.at[f, 0:1, ny + 1 : ny + 2]),
            copy(halo[5].at[f, 1:2], ext.at[f, nx + 1 : nx + 2, ny + 1 : ny + 2]),
        ]
        groups.append(moves + ([copy(mask_hbm, mask_ref)] if f == 0 else []))
    load_v = copy(v_hbm, v_ref)
    work, slot = [], 0
    for half, first, last in ((1, 0, count), (0, row, end)):
        pair = slice(2 * half, 2 * half + 2)
        for r in range(first, last, rows):
            there, here = slice(r, r + rows), slice(slot, slot + rows)
            slot += rows
            if half:
                n, at = (1, r) if r < row else ((0, r - row) if r < end else (2, r - end))
                moves = [copy(nows[n].at[:, at : at + rows], q_ref.at[:, there])]
            else:
                at = slice(r - row, r - row + rows)
                moves = [copy(prev_hbm.at[:, at], p_ref.at[:, at])]
            moves += [
                copy(flat_hbm.at[pair, there], feat_ref.at[:, here]),
                copy(cot_hbm.at[pair, there], cot_ref.at[:, here]),
            ]
            store = copy(up_ref.at[:, here], up_hbm.at[pair, there])
            work.append((half, r, here, moves, store))
    sent = [copy(agg_ref.at[f], agg_hbm.at[f]) for f in range(2)]
    for moves in groups:
        for move in moves:
            move.start()
    load_v.start()
    for item in work:
        for move in item[3]:
            move.start()
    slots = mask_ref.shape[2] // lipids
    for f in range(2):
        for move in groups[f]:
            move.wait()
        for x in range(nx):
            for y in range(ny):
                tile = x * ny + y
                parts = []
                for k in range(slots):
                    code = codes[tile * slots + k]
                    parts.append(ext[f, x + lax.div(code, 3), y + lax.rem(code, 3)])
                summed = jnp.dot(
                    mask_ref[tile],
                    jnp.concatenate(parts, axis=0),
                    preferred_element_type=F32,
                )
                agg_ref[f, tile * lipids : (tile + 1) * lipids] = (0.18 * summed).astype(BF16)
        sent[f].start()
    load_v.wait()
    for n, (half, r, here, moves, store) in enumerate(work):
        for move in moves:
            move.wait()
        there = slice(r, r + rows)
        mid = [agg_ref[0, there], agg_ref[1, there]]
        if half:
            before = mid + [q_ref[0, there], q_ref[1, there]]
        else:
            at = slice(r - row, r - row + rows)
            before = [p_ref[0, at], p_ref[1, at]] + mid
        updates, terms = chunk_terms(
            before,
            [feat_ref[f, here] for f in range(2)],
            [cot_ref[f, here] for f in range(2)],
            v_ref,
        )
        for f in range(2):
            up_ref[f, here] = updates[f]
        store.start()
        g_out[...] = terms if n == 0 else g_out[...] + terms
    for move in sent:
        move.wait()
    for item in work:
        item[4].wait()


def middle(row, codes, features, halo, mask, nows, prev, cotangent, v):
    frames, nx, ny, lipids, width = features.shape
    count = nx * ny * lipids
    flat = (frames, count, width)
    anywhere = pl.BlockSpec(memory_space=pl.ANY)
    some = 2 * count - 2 * row
    chunks = some // MIX_ROWS
    return pl.pallas_call(
        functools.partial(middle_kernel, row),
        in_specs=[pl.BlockSpec(memory_space=pltpu.SMEM)] + [anywhere] * 15,
        out_specs=[anywhere, anywhere, whole_vmem()],
        out_shape=[
            jax.ShapeDtypeStruct((2, count, width), BF16),
            jax.ShapeDtypeStruct(flat, BF16),
            jax.ShapeDtypeStruct(v.shape, F32),
        ],
        scratch_shapes=[
            pltpu.VMEM((2, nx + 2, ny + 2, lipids, width), BF16),
            pltpu.VMEM(mask.shape, BF16),
            pltpu.VMEM((2, count, width), BF16),
            pltpu.VMEM((2, count, width), BF16),
            pltpu.VMEM((2, count - 2 * row, width), BF16),
            pltpu.VMEM((2, some, width), BF16),
            pltpu.VMEM((2, some, width), BF16),
            pltpu.VMEM((2, some, width), BF16),
            pltpu.VMEM(v.shape, BF16),
            pltpu.SemaphoreType.DMA((22 + 4 * chunks,)),
        ],
        compiler_params=pltpu.CompilerParams(vmem_limit_bytes=VMEM),
        cost_estimate=pl.CostEstimate(flops=1, bytes_accessed=1, transcendentals=0),
        name="middle",
    )(
        codes,
        features,
        *halo,
        mask,
        *nows,
        prev,
        features.reshape(flat),
        cotangent,
        v,
    )


def finish_kernel(scale, g_ref, ws_ref, wt_ref, space_ref, time_ref):
    width = ws_ref.shape[0]
    space = jnp.zeros((width, width), F32)
    for j in range(wt_ref.shape[0]):
        g = g_ref[j * width : (j + 1) * width, :]
        high = g.astype(BF16)
        low = (g - high.astype(F32)).astype(BF16)
        time = 0.0
        for part in (low, high):
            time = time + lax.dot_general(
                ws_ref[...], part, (((0,), (0,)), ((), ())), preferred_element_type=F32
            )
            space = space + lax.dot_general(
                part, wt_ref[j], (((1,), (1,)), ((), ())), preferred_element_type=F32
            )
        time_ref[j] = time * scale
    space_ref[...] = space * scale


def finish(scale, total, w_space, w_time):
    return pl.pallas_call(
        functools.partial(finish_kernel, scale),
        in_specs=[whole_vmem()] * 3,
        out_specs=[whole_vmem()] * 2,
        out_shape=[
            jax.ShapeDtypeStruct(w_space.shape, F32),
            jax.ShapeDtypeStruct(w_time.shape, F32),
        ],
        compiler_params=pltpu.CompilerParams(vmem_limit_bytes=20 << 20),
        name="finish",
    )(total, w_space, w_time)


def all_sum(keep, give):
    half, width = keep.shape
    block, count = 8, lax.axis_size(REST)
    mine = keep + lax.ppermute(give, "core", ring(2, 1))
    mine = jnp.pad(mine, ((0, count * block - half), (0, 0)))
    mine = lax.all_to_all(mine.reshape(count, block, width), REST, 0, 0, tiled=True)
    spread = jnp.broadcast_to(mine.sum(axis=0)[None], (count, block, width))
    back = lax.all_to_all(spread, REST, 0, 0, tiled=True)
    back = back.reshape(count * block, width)[:half]
    other = lax.ppermute(back, "core", ring(2, 1))
    first = lax.axis_index("core") == 0
    return jnp.where(
        first, jnp.concatenate([back, other]), jnp.concatenate([other, back])
    )


def shards(features, neighbours, adjacency, w_space, w_time, cotangent):
    frames, nx, ny, lipids, width = features.shape
    count = nx * ny * lipids
    codes = neighbours.reshape(-1)
    up, down = ring(4, 1), ring(4, -1)
    onward = [(i, i + 1) for i in range(7)]
    inner, outer = tuple(range(1, nx - 1)), (0, nx - 1)

    every = slice(None)
    low, high = slice(0, 1), slice(ny - 1, ny)

    def exchange(axis, high_edge, low_edge):
        return lax.ppermute(high_edge, axis, up), lax.ppermute(low_edge, axis, down)

    def x_edges(source):
        edge = (frames, 1, ny, lipids, width)
        moves = [(0, (every, slice(nx - 1, nx)), 0, ()), (0, (every, low), 1, ())]
        return pack([source], [edge, edge], moves)

    def y_edges(first, source):
        edge = (2, nx, 1, lipids, width)
        pair = slice(first, first + 2)
        moves = [(0, (pair, every, side), o, ()) for o, side in enumerate((high, low))]
        return pack([source], [edge, edge], moves)

    def corner_edges(x_halo):
        corner = (2, 2, 1, lipids, width)
        moves = [
            (i, (slice(2 * p, 2 * p + 2), every, side), 2 * p + o, (every, slice(i, i + 1)))
            for i in range(2)
            for p in range(2)
            for o, side in enumerate((high, low))
        ]
        return pack(x_halo, [corner] * 4, moves)

    edges_x = x_edges(features)
    x_halo = exchange(GX, *edges_x)
    later, _ = lax.optimization_barrier((features, edges_x))
    edges_b = y_edges(2, later)
    y_b = exchange("gy", *edges_b)
    later, _ = lax.optimization_barrier((features, edges_b))
    edges_a = y_edges(0, later)
    y_a = exchange("gy", *edges_a)
    contacts = adjacency.reshape(nx * ny, -1, lipids, lipids)
    contacts, _ = lax.optimization_barrier((contacts, edges_b))
    mask, v = prep(contacts, w_space, w_time)
    (inner_b,) = aggregate(2, inner, codes, features, y_b, mask)
    x_halo, sent = lax.optimization_barrier((x_halo, inner_b))
    prev_inner = lax.ppermute(sent, "ta", onward)
    ends = corner_edges(x_halo)
    c_b = exchange("gy", *ends[2:])
    c_a = exchange("gy", *ends[:2])
    c_b, y_a = lax.optimization_barrier((c_b, y_a))
    outer_b = aggregate(2, outer, codes, features, (*y_b, *x_halo, *c_b), mask, 2)
    c_a, sent = lax.optimization_barrier((c_a, outer_b))
    prev_first = lax.ppermute(sent[0], "ta", onward)
    prev_last = lax.ppermute(sent[1], "ta", onward)
    feat = features.reshape(frames, count, width)
    cot = cotangent.reshape(frames, count, width)
    a_row = ny * lipids
    end = count - a_row
    agg_a, updated, total = middle(
        a_row,
        codes,
        features,
        (*y_a, *x_halo, *c_a),
        mask,
        (inner_b, *outer_b),
        prev_inner,
        cot,
        v,
    )
    updated, total = mix(
        0,
        [(0, r, 0, r, r) for r in range(0, a_row, MIX_ROWS)],
        [prev_first],
        [agg_a],
        feat,
        cot,
        v,
        (total, updated),
    )
    me = lax.axis_index("core").reshape(1)
    updated, keep, give = mix(
        0,
        [(0, r - end, 0, r, r) for r in range(end, count, MIX_ROWS)],
        [prev_last],
        [agg_a],
        feat,
        cot,
        v,
        (total, updated),
        me,
    )
    total = all_sum(keep, give)
    scale = 1.0 / math.sqrt(frames * count * lax.axis_size(EVERY))
    grad_space, grad_time = finish(scale, total, w_space, w_time)
    return updated.reshape(features.shape), grad_space, grad_time


def solution(mesh):
    gx, gy, ta = (mesh.shape[a] for a in ("gx", "gy", "ta"))
    fine = Mesh(
        np.asarray(mesh.devices).reshape(2, gx // 2, gy, ta), ("yh", "core", "gy", "ta")
    )
    in_specs = (
        P("ta", GX, "gy", None, None),
        P(GX, "gy", None),
        P(GX, "gy", None, None, None),
        P(),
        P(),
        P("ta", GX, "gy", None, None),
    )
    out_specs = (P("ta", GX, "gy", None, None), P(), P())
    return jax.shard_map(shards, mesh=fine, in_specs=in_specs, out_specs=out_specs, check_vma=False)
```

```python
import functools
import math

import jax
import jax.numpy as jnp
import numpy as np
from jax import lax
from jax.experimental import pallas as pl
from jax.experimental.pallas import tpu as pltpu
from jax.sharding import Mesh
from jax.sharding import PartitionSpec as P

BF16 = jnp.bfloat16
F32 = jnp.float32
GX = ("yh", "core")
MIX_ROWS = 256
VMEM = 65300 << 10
EVERY = ("yh", "core", "gy", "ta")
REST = ("yh", "gy", "ta")


def ring(count, step):
    return [(i, (i + step) % count) for i in range(count)]


def whole_vmem():
    return pl.BlockSpec(memory_space=pltpu.VMEM)


def prep_kernel(adj_ref, ws_ref, wt_ref, mask_ref, v_ref):
    slots, lipids = adj_ref.shape[1], adj_ref.shape[2]
    width = ws_ref.shape[1]
    for t in range(adj_ref.shape[0]):
        for k in range(slots):
            mask_ref[t, :, k * lipids : (k + 1) * lipids] = (
                adj_ref[t, k].astype(F32).astype(BF16)
            )

    @pl.when(pl.program_id(0) == 0)
    def _():
        for j in range(wt_ref.shape[0]):
            v_ref[j * width : (j + 1) * width, :] = jnp.dot(
                ws_ref[...], wt_ref[j], preferred_element_type=F32
            ).astype(BF16)


def prep(adjacency, w_space, w_time):
    tiles, slots, lipids, _ = adjacency.shape
    taps, width, _ = w_time.shape
    return pl.pallas_call(
        prep_kernel,
        grid=(tiles // 4,),
        in_specs=[
            pl.BlockSpec((4, slots, lipids, lipids), lambda i: (i, 0, 0, 0)),
            pl.BlockSpec((width, width), lambda i: (0, 0)),
            pl.BlockSpec((taps, width, width), lambda i: (0, 0, 0)),
        ],
        out_specs=[
            pl.BlockSpec((4, lipids, slots * lipids), lambda i: (i, 0, 0)),
            pl.BlockSpec((taps * width, width), lambda i: (0, 0)),
        ],
        out_shape=[
            jax.ShapeDtypeStruct((tiles, lipids, slots * lipids), BF16),
            jax.ShapeDtypeStruct((taps * width, width), BF16),
        ],
        compiler_params=pltpu.CompilerParams(vmem_limit_bytes=VMEM),
        cost_estimate=pl.CostEstimate(
            flops=2 * taps * width**3, bytes_accessed=8 << 20, transcendentals=0
        ),
        name="prep",
    )(adjacency, w_space, w_time)


def pack_kernel(moves, count, *refs):
    *arrays, sems = refs
    copies = [
        pltpu.make_async_copy(arrays[i].at[src], arrays[count + o].at[dst], sems.at[n])
        for n, (i, src, o, dst) in enumerate(moves)
    ]
    for copy in copies:
        copy.start()
    for copy in copies:
        copy.wait()


def pack(arrays, shapes, moves):
    anywhere = pl.BlockSpec(memory_space=pl.ANY)
    return pl.pallas_call(
        functools.partial(pack_kernel, moves, len(arrays)),
        in_specs=[anywhere] * len(arrays),
        out_specs=[whole_vmem()] * len(shapes),
        out_shape=[jax.ShapeDtypeStruct(shape, BF16) for shape in shapes],
        scratch_shapes=[pltpu.SemaphoreType.DMA((len(moves),))],
        compiler_params=pltpu.CompilerParams(vmem_limit_bytes=VMEM),
        cost_estimate=pl.CostEstimate(flops=0, bytes_accessed=6 << 20, transcendentals=0),
        name="pack",
    )(*arrays)


def agg_kernel(first, xs, edge, pieces, codes, feat, *rest):
    *ins, ext, mask_ref, out_ref, sems = rest
    halo, mask_hbm, outs = ins[: -pieces - 1], ins[-pieces - 1], ins[-pieces:]
    frames, _, ny = out_ref.shape[:3]
    nx = feat.shape[1]
    inside = slice(edge, nx + edge)
    groups = []
    for f in range(frames):
        moves = [
            (feat.at[first + f], ext.at[f, inside, 1 : ny + 1]),
            (halo[0].at[f], ext.at[f, inside, 0:1]),
            (halo[1].at[f], ext.at[f, inside, ny + 1 : ny + 2]),
        ]
        if f == 0:
            moves += [
                (mask_hbm.at[x * ny : (x + 1) * ny], mask_ref.at[i * ny : (i + 1) * ny])
                for i, x in enumerate(xs)
            ]
        if edge:
            xlo, xhi = (ref.at[first + f] for ref in halo[2:4])
            clo, chi = (ref.at[f] for ref in halo[4:])
            moves += [
                (xlo, ext.at[f, 0:1, 1 : ny + 1]),
                (xhi, ext.at[f, nx + 1 : nx + 2, 1 : ny + 1]),
                (clo.at[0:1], ext.at[f, 0:1, 0:1]),
                (clo.at[1:2], ext.at[f, nx + 1 : nx + 2, 0:1]),
                (chi.at[0:1], ext.at[f, 0:1, ny + 1 : ny + 2]),
                (chi.at[1:2], ext.at[f, nx + 1 : nx + 2, ny + 1 : ny + 2]),
            ]
        groups.append(moves)
    copies, used = [], 0
    for moves in groups:
        copies.append(
            [
                pltpu.make_async_copy(src, dst, sems.at[used + i])
                for i, (src, dst) in enumerate(moves)
            ]
        )
        used += len(moves)
        for copy in copies[-1]:
            copy.start()
    slots = mask_ref.shape[2] // mask_ref.shape[1]
    sent = []
    for f in range(frames):
        for copy in copies[f]:
            copy.wait()
        for i, x in enumerate(xs):
            for y in range(ny):
                places = []
                for k in range(slots):
                    code = codes[(x * ny + y) * slots + k]
                    places.append(
                        (x - 1 + edge + lax.div(code, 3), y + lax.rem(code, 3))
                    )
                source = jnp.concatenate([ext[f, sx, sy] for sx, sy in places], axis=0)
                summed = jnp.dot(
                    mask_ref[i * ny + y], source, preferred_element_type=F32
                )
                out_ref[f, i, y] = (0.18 * summed).astype(BF16)
        piece = len(xs) // pieces
        for n, out in enumerate(outs):
            rows = slice(n * piece, (n + 1) * piece)
            copy = pltpu.make_async_copy(
                out_ref.at[f, rows], out.at[f], sems.at[used + f * pieces + n]
            )
            copy.start()
            sent.append(copy)
    for copy in sent:
        copy.wait()


def aggregate(first, xs, codes, features, halo, mask, pieces=1):
    _, nx, ny, lipids, width = features.shape
    frames = 2
    slots = mask.shape[2] // lipids
    edge = 1 if len(halo) > 2 else 0
    anywhere = pl.BlockSpec(memory_space=pl.ANY)
    flops = 2 * frames * len(xs) * ny * lipids * mask.shape[2] * width
    out_shape = (frames, len(xs), ny, lipids, width)
    out = pl.pallas_call(
        functools.partial(agg_kernel, first, xs, edge, pieces),
        in_specs=[pl.BlockSpec(memory_space=pltpu.SMEM)] + [anywhere] * (len(halo) + 2),
        out_specs=[anywhere] * pieces,
        out_shape=[
            jax.ShapeDtypeStruct(
                (frames, len(xs) // pieces, ny, lipids, width), BF16
            )
        ]
        * pieces,
        scratch_shapes=[
            pltpu.VMEM((frames, nx + 2 * edge, ny + 2, lipids, width), BF16),
            pltpu.VMEM((len(xs) * ny, lipids, slots * lipids), BF16),
            pltpu.VMEM(out_shape, BF16),
            pltpu.SemaphoreType.DMA((frames * (12 + len(xs)),)),
        ],
        compiler_params=pltpu.CompilerParams(vmem_limit_bytes=VMEM),
        cost_estimate=pl.CostEstimate(
            flops=flops, bytes_accessed=8 << 20, transcendentals=0
        ),
        name="aggregate",
    )(codes, features, *halo, mask)
    return [piece.reshape(frames, -1, width) for piece in out]


def chunk_terms(before, features, cotangents, v_ref):
    lefts, grads, updates = [], [], []
    for f in range(2):
        left = jnp.concatenate([before[f + 2], before[f + 1], before[f]], axis=1)
        mixed = jnp.dot(left, v_ref[...], preferred_element_type=F32)
        s = 0.5 * jnp.tanh(0.5 * mixed) + 0.5
        silu = mixed * s
        updates.append((features[f].astype(F32) + silu).astype(BF16))
        grad = cotangents[f].astype(F32) * (s + silu * (1.0 - s))
        lefts.append(left)
        grads.append(grad.astype(BF16))
    terms = lax.dot_general(
        jnp.concatenate(lefts, axis=0),
        jnp.concatenate(grads, axis=0),
        (((0,), (0,)), ((), ())),
        preferred_element_type=F32,
    )
    return updates, terms


def mix_kernel(half, chunks, sizes, final, *refs):
    n_prev, n_now = sizes
    prevs, nows = refs[:n_prev], refs[n_prev : n_prev + n_now]
    feat_hbm, cot_hbm, v_hbm, *refs = refs[n_prev + n_now :]
    *refs, p_ref, q_ref, feat_ref, cot_ref, v_ref, up_ref, g_ref, given_ref, sems = refs
    given = refs[0] if half == 0 else None
    up_hbm, outs = refs[-2 - final], refs[-1 - final :]
    rows, count = MIX_ROWS, len(chunks)
    pair = slice(2 * half, 2 * half + 2)
    first = pltpu.make_async_copy(v_hbm, v_ref, sems.at[0])
    last = pltpu.make_async_copy(given, given_ref, sems.at[1]) if given is not None else None
    loads, stores = [], []
    for c, (p, p_row, q, q_row, place) in enumerate(chunks):
        here, there = slice(c * rows, (c + 1) * rows), slice(place, place + rows)
        moves = (
            (nows[q].at[:, q_row : q_row + rows], q_ref),
            (prevs[p].at[:, p_row : p_row + rows], p_ref),
            (feat_hbm.at[pair, there], feat_ref),
            (cot_hbm.at[pair, there], cot_ref),
        )
        loads.append(
            [
                pltpu.make_async_copy(src, dst.at[:, here], sems.at[2 + 5 * c + i])
                for i, (src, dst) in enumerate(moves)
            ]
        )
        stores.append(
            pltpu.make_async_copy(
                up_ref.at[:, here], up_hbm.at[pair, there], sems.at[2 + 5 * c + 4]
            )
        )
    first.start()
    for copy in sum(loads, []):
        copy.start()
    if last is not None:
        last.start()
    first.wait()
    for c in range(count):
        for copy in loads[c]:
            copy.wait()
        here = slice(c * rows, (c + 1) * rows)
        before = [p_ref[0, here], p_ref[1, here], q_ref[0, here], q_ref[1, here]]
        updates, terms = chunk_terms(
            before,
            [feat_ref[f, here] for f in range(2)],
            [cot_ref[f, here] for f in range(2)],
            v_ref,
        )
        for f in range(2):
            up_ref[f, here] = updates[f]
        stores[c].start()
        g_ref[...] = terms if c == 0 else g_ref[...] + terms
    if last is not None:
        last.wait()
    if final:
        me = refs[1][0]
        share = g_ref.shape[0] // 2
        low, high = slice(0, share), slice(share, 2 * share)
        for core, (mine, theirs) in enumerate(((low, high), (high, low))):

            @pl.when(me == core)
            def _(mine=mine, theirs=theirs):
                outs[0][...] = g_ref[mine] + given_ref[mine]
                outs[1][...] = g_ref[theirs] + given_ref[theirs]

    else:
        outs[0][...] = g_ref[...] + given_ref[...] if last is not None else g_ref[...]
    for copy in stores:
        copy.wait()


def mix(half, chunks, prevs, nows, features, cotangent, v, given=None, me=None):
    frames, width = 2, v.shape[1]
    anywhere = pl.BlockSpec(memory_space=pl.ANY)
    block = pltpu.VMEM((frames, len(chunks) * MIX_ROWS, width), BF16)
    sums = jax.ShapeDtypeStruct(v.shape, F32)
    share = jax.ShapeDtypeStruct((v.shape[0] // 2, width), F32)
    arrays = [*prevs, *nows, features, cotangent, v]
    specs = [anywhere] * len(arrays)
    aliases = {}
    if given is not None:
        final = 1 if me is not None else 0
        total, updated = given
        core = me if final else jnp.zeros((1,), jnp.int32)
        arrays += [total, core, updated]
        aliases = {len(arrays) - 1: 0}
        specs += [anywhere, pl.BlockSpec(memory_space=pltpu.SMEM), anywhere]
    else:
        final = 0
    return pl.pallas_call(
        functools.partial(mix_kernel, half, chunks, (len(prevs), len(nows)), final),
        in_specs=specs,
        out_specs=[anywhere] + [whole_vmem()] * (1 + final),
        out_shape=[jax.ShapeDtypeStruct(features.shape, BF16)]
        + ([share, share] if final else [sums]),
        scratch_shapes=[block] * 4
        + [
            pltpu.VMEM(v.shape, BF16),
            block,
            pltpu.VMEM(v.shape, F32),
            pltpu.VMEM(v.shape, F32),
            pltpu.SemaphoreType.DMA((2 + 5 * len(chunks),)),
        ],
        input_output_aliases=aliases,
        compiler_params=pltpu.CompilerParams(vmem_limit_bytes=VMEM),
        cost_estimate=pl.CostEstimate(flops=1, bytes_accessed=1, transcendentals=0),
        name="mix",
    )(*arrays)


def middle_kernel(row, codes, feat, *refs):
    ins, scratch = refs[:16], refs[16:]
    halo, mask_hbm, nows = ins[:6], ins[6], ins[7:10]
    prev_hbm, flat_hbm, cot_hbm, v_hbm, agg_hbm, up_hbm = ins[10:]
    g_out, ext, mask_ref, agg_ref, q_ref, p_ref, feat_ref, cot_ref, up_ref, v_ref, sems = scratch
    _, nx, ny, lipids, _ = feat.shape
    count, rows = nx * ny * lipids, MIX_ROWS
    end = count - row
    used = [0]

    def copy(src, dst):
        used[0] += 1
        return pltpu.make_async_copy(src, dst, sems.at[used[0] - 1])

    groups = []
    for f in range(2):
        moves = [
            copy(feat.at[f], ext.at[f, 1 : nx + 1, 1 : ny + 1]),
            copy(halo[0].at[f], ext.at[f, 1 : nx + 1, 0:1]),
            copy(halo[1].at[f], ext.at[f, 1 : nx + 1, ny + 1 : ny + 2]),
            copy(halo[2].at[f], ext.at[f, 0:1, 1 : ny + 1]),
            copy(halo[3].at[f], ext.at[f, nx + 1 : nx + 2, 1 : ny + 1]),
            copy(halo[4].at[f, 0:1], ext.at[f, 0:1, 0:1]),
            copy(halo[4].at[f, 1:2], ext.at[f, nx + 1 : nx + 2, 0:1]),
            copy(halo[5].at[f, 0:1], ext.at[f, 0:1, ny + 1 : ny + 2]),
            copy(halo[5].at[f, 1:2], ext.at[f, nx + 1 : nx + 2, ny + 1 : ny + 2]),
        ]
        groups.append(moves)
    masks = [
        copy(mask_hbm.at[x * ny : (x + 1) * ny], mask_ref.at[x * ny : (x + 1) * ny])
        for x in range(nx)
    ]
    load_v = copy(v_hbm, v_ref)
    work, slot = [], 0
    for half, first, last in ((1, 0, count), (0, row, end)):
        pair = slice(2 * half, 2 * half + 2)
        for r in range(first, last, rows):
            there, here = slice(r, r + rows), slice(slot, slot + rows)
            slot += rows
            if half:
                n, at = (1, r) if r < row else ((0, r - row) if r < end else (2, r - end))
                moves = [copy(nows[n].at[:, at : at + rows], q_ref.at[:, there])]
            else:
                at = slice(r - row, r - row + rows)
                moves = [copy(prev_hbm.at[:, at], p_ref.at[:, at])]
            moves.append(copy(cot_hbm.at[pair, there], cot_ref.at[:, here]))
            if half:
                moves.append(copy(flat_hbm.at[pair, there], feat_ref.at[:, there]))
            store = copy(up_ref.at[:, here], up_hbm.at[pair, there])
            work.append((half, r, here, moves, store))
    sent = [copy(agg_ref.at[f], agg_hbm.at[f]) for f in range(2)]
    for moves in (groups[0], masks, groups[1]):
        for move in moves:
            move.start()
    load_v.start()
    for item in work:
        for move in item[3]:
            move.start()
    slots = mask_ref.shape[2] // lipids
    for f in range(2):
        for move in groups[f]:
            move.wait()
        for x in range(nx):
            if f == 0:
                masks[x].wait()
            for y in range(ny):
                tile = x * ny + y
                parts = []
                for k in range(slots):
                    code = codes[tile * slots + k]
                    parts.append(ext[f, x + lax.div(code, 3), y + lax.rem(code, 3)])
                summed = jnp.dot(
                    mask_ref[tile],
                    jnp.concatenate(parts, axis=0),
                    preferred_element_type=F32,
                )
                agg_ref[f, tile * lipids : (tile + 1) * lipids] = (0.18 * summed).astype(BF16)
        sent[f].start()
    load_v.wait()
    for n, (half, r, here, moves, store) in enumerate(work):
        for move in moves:
            move.wait()
        there = slice(r, r + rows)
        mid = [agg_ref[0, there], agg_ref[1, there]]
        if half:
            before = mid + [q_ref[0, there], q_ref[1, there]]
            own = [feat_ref[f, there] for f in range(2)]
        else:
            tiles = [divmod(t // lipids, ny) for t in range(r, r + rows, lipids)]
            own = [
                jnp.concatenate([ext[f, x + 1, y + 1] for x, y in tiles], axis=0)
                for f in range(2)
            ]
            at = slice(r - row, r - row + rows)
            before = [p_ref[0, at], p_ref[1, at]] + mid
        updates, terms = chunk_terms(
            before, own, [cot_ref[f, here] for f in range(2)], v_ref
        )
        for f in range(2):
            up_ref[f, here] = updates[f]
        store.start()
        g_out[...] = terms if n == 0 else g_out[...] + terms
    for move in sent:
        move.wait()
    for item in work:
        item[4].wait()


def middle(row, codes, features, halo, mask, nows, prev, cotangent, v):
    frames, nx, ny, lipids, width = features.shape
    count = nx * ny * lipids
    flat = (frames, count, width)
    anywhere = pl.BlockSpec(memory_space=pl.ANY)
    some = 2 * count - 2 * row
    chunks = some // MIX_ROWS
    return pl.pallas_call(
        functools.partial(middle_kernel, row),
        in_specs=[pl.BlockSpec(memory_space=pltpu.SMEM)] + [anywhere] * 15,
        out_specs=[anywhere, anywhere, whole_vmem()],
        out_shape=[
            jax.ShapeDtypeStruct((2, count, width), BF16),
            jax.ShapeDtypeStruct(flat, BF16),
            jax.ShapeDtypeStruct(v.shape, F32),
        ],
        scratch_shapes=[
            pltpu.VMEM((2, nx + 2, ny + 2, lipids, width), BF16),
            pltpu.VMEM(mask.shape, BF16),
            pltpu.VMEM((2, count, width), BF16),
            pltpu.VMEM((2, count, width), BF16),
            pltpu.VMEM((2, count - 2 * row, width), BF16),
            pltpu.VMEM((2, count, width), BF16),
            pltpu.VMEM((2, some, width), BF16),
            pltpu.VMEM((2, some, width), BF16),
            pltpu.VMEM(v.shape, BF16),
            pltpu.SemaphoreType.DMA((25 + 4 * chunks,)),
        ],
        compiler_params=pltpu.CompilerParams(vmem_limit_bytes=VMEM),
        cost_estimate=pl.CostEstimate(flops=1, bytes_accessed=1, transcendentals=0),
        name="middle",
    )(
        codes,
        features,
        *halo,
        mask,
        *nows,
        prev,
        features.reshape(flat),
        cotangent,
        v,
    )


def finish_kernel(scale, g_ref, ws_ref, wt_ref, space_ref, time_ref):
    width = ws_ref.shape[0]
    space = jnp.zeros((width, width), F32)
    for j in range(wt_ref.shape[0]):
        g = g_ref[j * width : (j + 1) * width, :]
        high = g.astype(BF16)
        low = (g - high.astype(F32)).astype(BF16)
        time = 0.0
        for part in (low, high):
            time = time + lax.dot_general(
                ws_ref[...], part, (((0,), (0,)), ((), ())), preferred_element_type=F32
            )
            space = space + lax.dot_general(
                part, wt_ref[j], (((1,), (1,)), ((), ())), preferred_element_type=F32
            )
        time_ref[j] = time * scale
    space_ref[...] = space * scale


def finish(scale, total, w_space, w_time):
    return pl.pallas_call(
        functools.partial(finish_kernel, scale),
        in_specs=[whole_vmem()] * 3,
        out_specs=[whole_vmem()] * 2,
        out_shape=[
            jax.ShapeDtypeStruct(w_space.shape, F32),
            jax.ShapeDtypeStruct(w_time.shape, F32),
        ],
        compiler_params=pltpu.CompilerParams(vmem_limit_bytes=20 << 20),
        name="finish",
    )(total, w_space, w_time)


def all_sum(keep, give):
    half, width = keep.shape
    block, count = 8, lax.axis_size(REST)
    mine = keep + lax.ppermute(give, "core", ring(2, 1))
    mine = jnp.pad(mine, ((0, count * block - half), (0, 0)))
    mine = lax.all_to_all(mine.reshape(count, block, width), REST, 0, 0, tiled=True)
    spread = jnp.broadcast_to(mine.sum(axis=0)[None], (count, block, width))
    back = lax.all_to_all(spread, REST, 0, 0, tiled=True)
    back = back.reshape(count * block, width)[:half]
    other = lax.ppermute(back, "core", ring(2, 1))
    first = lax.axis_index("core") == 0
    return jnp.where(
        first, jnp.concatenate([back, other]), jnp.concatenate([other, back])
    )


def shards(features, neighbours, adjacency, w_space, w_time, cotangent):
    frames, nx, ny, lipids, width = features.shape
    count = nx * ny * lipids
    codes = neighbours.reshape(-1)
    up, down = ring(4, 1), ring(4, -1)
    onward = [(i, i + 1) for i in range(7)]
    inner, outer = tuple(range(1, nx - 1)), (0, nx - 1)

    every = slice(None)
    low, high = slice(0, 1), slice(ny - 1, ny)

    def exchange(axis, high_edge, low_edge):
        return lax.ppermute(high_edge, axis, up), lax.ppermute(low_edge, axis, down)

    def x_edges(source):
        edge = (frames, 1, ny, lipids, width)
        moves = [(0, (every, slice(nx - 1, nx)), 0, ()), (0, (every, low), 1, ())]
        return pack([source], [edge, edge], moves)

    def y_edges(first, source):
        edge = (2, nx, 1, lipids, width)
        pair = slice(first, first + 2)
        moves = [(0, (pair, every, side), o, ()) for o, side in enumerate((high, low))]
        return pack([source], [edge, edge], moves)

    def corner_edges(x_halo):
        corner = (2, 2, 1, lipids, width)
        moves = [
            (i, (slice(2 * p, 2 * p + 2), every, side), 2 * p + o, (every, slice(i, i + 1)))
            for i in range(2)
            for p in range(2)
            for o, side in enumerate((high, low))
        ]
        return pack(x_halo, [corner] * 4, moves)

    edges_x = x_edges(features)
    x_halo = exchange(GX, *edges_x)
    later, _ = lax.optimization_barrier((features, edges_x))
    edges_b = y_edges(2, later)
    y_b = exchange("gy", *edges_b)
    contacts = adjacency.reshape(nx * ny, -1, lipids, lipids)
    contacts, _ = lax.optimization_barrier((contacts, edges_b))
    mask, v = prep(contacts, w_space, w_time)
    later, _ = lax.optimization_barrier((features, mask))
    edges_a = y_edges(0, later)
    y_a = exchange("gy", *edges_a)
    (inner_b,) = aggregate(2, inner, codes, features, y_b, mask)
    x_halo, sent = lax.optimization_barrier((x_halo, inner_b))
    prev_inner = lax.ppermute(sent, "ta", onward)
    ends = corner_edges(x_halo)
    c_b = exchange("gy", *ends[2:])
    c_a = exchange("gy", *ends[:2])
    c_b, y_a = lax.optimization_barrier((c_b, y_a))
    outer_b = aggregate(2, outer, codes, features, (*y_b, *x_halo, *c_b), mask, 2)
    c_a, sent = lax.optimization_barrier((c_a, outer_b))
    prev_first = lax.ppermute(sent[0], "ta", onward)
    prev_last = lax.ppermute(sent[1], "ta", onward)
    feat = features.reshape(frames, count, width)
    cot = cotangent.reshape(frames, count, width)
    a_row = ny * lipids
    end = count - a_row
    agg_a, updated, total = middle(
        a_row,
        codes,
        features,
        (*y_a, *x_halo, *c_a),
        mask,
        (inner_b, *outer_b),
        prev_inner,
        cot,
        v,
    )
    updated, total = mix(
        0,
        [(0, r, 0, r, r) for r in range(0, a_row, MIX_ROWS)],
        [prev_first],
        [agg_a],
        feat,
        cot,
        v,
        (total, updated),
    )
    me = lax.axis_index("core").reshape(1)
    updated, keep, give = mix(
        0,
        [(0, r - end, 0, r, r) for r in range(end, count, MIX_ROWS)],
        [prev_last],
        [agg_a],
        feat,
        cot,
        v,
        (total, updated),
        me,
    )
    total = all_sum(keep, give)
    scale = 1.0 / math.sqrt(frames * count * lax.axis_size(EVERY))
    grad_space, grad_time = finish(scale, total, w_space, w_time)
    return updated.reshape(features.shape), grad_space, grad_time


def solution(mesh):
    gx, gy, ta = (mesh.shape[a] for a in ("gx", "gy", "ta"))
    fine = Mesh(
        np.asarray(mesh.devices).reshape(2, gx // 2, gy, ta), ("yh", "core", "gy", "ta")
    )
    in_specs = (
        P("ta", GX, "gy", None, None),
        P(GX, "gy", None),
        P(GX, "gy", None, None, None),
        P(),
        P(),
        P("ta", GX, "gy", None, None),
    )
    out_specs = (P("ta", GX, "gy", None, None), P(), P())
    return jax.shard_map(shards, mesh=fine, in_specs=in_specs, out_specs=out_specs, check_vma=False)
```

```python
import functools
import math

import jax
import jax.numpy as jnp
import numpy as np
from jax import lax
from jax.experimental import pallas as pl
from jax.experimental.pallas import tpu as pltpu
from jax.sharding import Mesh
from jax.sharding import PartitionSpec as P

BF16 = jnp.bfloat16
F32 = jnp.float32
GX = ("yh", "core")
MIX_ROWS = 256
VMEM = 65300 << 10
EVERY = ("yh", "core", "gy", "ta")
REST = ("yh", "gy", "ta")


def ring(count, step):
    return [(i, (i + step) % count) for i in range(count)]


def whole_vmem():
    return pl.BlockSpec(memory_space=pltpu.VMEM)


def prep_kernel(adj_ref, ws_ref, wt_ref, mask_ref, v_ref):
    slots, lipids = adj_ref.shape[1], adj_ref.shape[2]
    width = ws_ref.shape[1]
    for t in range(adj_ref.shape[0]):
        for k in range(slots):
            mask_ref[t, :, k * lipids : (k + 1) * lipids] = (
                adj_ref[t, k].astype(F32).astype(BF16)
            )

    @pl.when(pl.program_id(0) == 0)
    def _():
        for j in range(wt_ref.shape[0]):
            v_ref[j * width : (j + 1) * width, :] = jnp.dot(
                ws_ref[...], wt_ref[j], preferred_element_type=F32
            ).astype(BF16)


def prep(adjacency, w_space, w_time):
    tiles, slots, lipids, _ = adjacency.shape
    taps, width, _ = w_time.shape
    return pl.pallas_call(
        prep_kernel,
        grid=(tiles // 4,),
        in_specs=[
            pl.BlockSpec((4, slots, lipids, lipids), lambda i: (i, 0, 0, 0)),
            pl.BlockSpec((width, width), lambda i: (0, 0)),
            pl.BlockSpec((taps, width, width), lambda i: (0, 0, 0)),
        ],
        out_specs=[
            pl.BlockSpec((4, lipids, slots * lipids), lambda i: (i, 0, 0)),
            pl.BlockSpec((taps * width, width), lambda i: (0, 0)),
        ],
        out_shape=[
            jax.ShapeDtypeStruct((tiles, lipids, slots * lipids), BF16),
            jax.ShapeDtypeStruct((taps * width, width), BF16),
        ],
        compiler_params=pltpu.CompilerParams(vmem_limit_bytes=VMEM),
        cost_estimate=pl.CostEstimate(
            flops=2 * taps * width**3, bytes_accessed=8 << 20, transcendentals=0
        ),
        name="prep",
    )(adjacency, w_space, w_time)


def pack_kernel(moves, count, *refs):
    *arrays, sems = refs
    copies = [
        pltpu.make_async_copy(arrays[i].at[src], arrays[count + o].at[dst], sems.at[n])
        for n, (i, src, o, dst) in enumerate(moves)
    ]
    for copy in copies:
        copy.start()
    for copy in copies:
        copy.wait()


def pack(arrays, shapes, moves):
    anywhere = pl.BlockSpec(memory_space=pl.ANY)
    return pl.pallas_call(
        functools.partial(pack_kernel, moves, len(arrays)),
        in_specs=[anywhere] * len(arrays),
        out_specs=[whole_vmem()] * len(shapes),
        out_shape=[jax.ShapeDtypeStruct(shape, BF16) for shape in shapes],
        scratch_shapes=[pltpu.SemaphoreType.DMA((len(moves),))],
        compiler_params=pltpu.CompilerParams(vmem_limit_bytes=VMEM),
        cost_estimate=pl.CostEstimate(flops=0, bytes_accessed=6 << 20, transcendentals=0),
        name="pack",
    )(*arrays)


def agg_kernel(first, xs, edge, pieces, codes, feat, *rest):
    *ins, ext, mask_ref, out_ref, sems = rest
    halo, mask_hbm, outs = ins[: -pieces - 1], ins[-pieces - 1], ins[-pieces:]
    frames, _, ny = out_ref.shape[:3]
    nx = feat.shape[1]
    inside = slice(edge, nx + edge)
    groups = []
    for f in range(frames):
        moves = [
            (feat.at[first + f], ext.at[f, inside, 1 : ny + 1]),
            (halo[0].at[f], ext.at[f, inside, 0:1]),
            (halo[1].at[f], ext.at[f, inside, ny + 1 : ny + 2]),
        ]
        if f == 0:
            moves += [
                (mask_hbm.at[x * ny : (x + 1) * ny], mask_ref.at[i * ny : (i + 1) * ny])
                for i, x in enumerate(xs)
            ]
        if edge:
            xlo, xhi = (ref.at[first + f] for ref in halo[2:4])
            clo, chi = (ref.at[f] for ref in halo[4:])
            moves += [
                (xlo, ext.at[f, 0:1, 1 : ny + 1]),
                (xhi, ext.at[f, nx + 1 : nx + 2, 1 : ny + 1]),
                (clo.at[0:1], ext.at[f, 0:1, 0:1]),
                (clo.at[1:2], ext.at[f, nx + 1 : nx + 2, 0:1]),
                (chi.at[0:1], ext.at[f, 0:1, ny + 1 : ny + 2]),
                (chi.at[1:2], ext.at[f, nx + 1 : nx + 2, ny + 1 : ny + 2]),
            ]
        groups.append(moves)
    copies, used = [], 0
    for moves in groups:
        copies.append(
            [
                pltpu.make_async_copy(src, dst, sems.at[used + i])
                for i, (src, dst) in enumerate(moves)
            ]
        )
        used += len(moves)
        for copy in copies[-1]:
            copy.start()
    slots = mask_ref.shape[2] // mask_ref.shape[1]
    sent = []
    for f in range(frames):
        for copy in copies[f]:
            copy.wait()
        for i, x in enumerate(xs):
            for y in range(ny):
                places = []
                for k in range(slots):
                    code = codes[(x * ny + y) * slots + k]
                    places.append(
                        (x - 1 + edge + lax.div(code, 3), y + lax.rem(code, 3))
                    )
                source = jnp.concatenate([ext[f, sx, sy] for sx, sy in places], axis=0)
                summed = jnp.dot(
                    mask_ref[i * ny + y], source, preferred_element_type=F32
                )
                out_ref[f, i, y] = (0.18 * summed).astype(BF16)
        piece = len(xs) // pieces
        for n, out in enumerate(outs):
            rows = slice(n * piece, (n + 1) * piece)
            copy = pltpu.make_async_copy(
                out_ref.at[f, rows], out.at[f], sems.at[used + f * pieces + n]
            )
            copy.start()
            sent.append(copy)
    for copy in sent:
        copy.wait()


def aggregate(first, xs, codes, features, halo, mask, pieces=1):
    _, nx, ny, lipids, width = features.shape
    frames = 2
    slots = mask.shape[2] // lipids
    edge = 1 if len(halo) > 2 else 0
    anywhere = pl.BlockSpec(memory_space=pl.ANY)
    flops = 2 * frames * len(xs) * ny * lipids * mask.shape[2] * width
    out_shape = (frames, len(xs), ny, lipids, width)
    out = pl.pallas_call(
        functools.partial(agg_kernel, first, xs, edge, pieces),
        in_specs=[pl.BlockSpec(memory_space=pltpu.SMEM)] + [anywhere] * (len(halo) + 2),
        out_specs=[anywhere] * pieces,
        out_shape=[
            jax.ShapeDtypeStruct(
                (frames, len(xs) // pieces, ny, lipids, width), BF16
            )
        ]
        * pieces,
        scratch_shapes=[
            pltpu.VMEM((frames, nx + 2 * edge, ny + 2, lipids, width), BF16),
            pltpu.VMEM((len(xs) * ny, lipids, slots * lipids), BF16),
            pltpu.VMEM(out_shape, BF16),
            pltpu.SemaphoreType.DMA((frames * (12 + len(xs)),)),
        ],
        compiler_params=pltpu.CompilerParams(vmem_limit_bytes=VMEM),
        cost_estimate=pl.CostEstimate(
            flops=flops, bytes_accessed=8 << 20, transcendentals=0
        ),
        name="aggregate",
    )(codes, features, *halo, mask)
    return [piece.reshape(frames, -1, width) for piece in out]


def chunk_terms(before, features, cotangents, v_ref):
    lefts, grads, updates = [], [], []
    for f in range(2):
        left = jnp.concatenate([before[f + 2], before[f + 1], before[f]], axis=1)
        mixed = jnp.dot(left, v_ref[...], preferred_element_type=F32)
        s = 0.5 * jnp.tanh(0.5 * mixed) + 0.5
        silu = mixed * s
        updates.append((features[f].astype(F32) + silu).astype(BF16))
        grad = cotangents[f].astype(F32) * (s + silu * (1.0 - s))
        lefts.append(left)
        grads.append(grad.astype(BF16))
    terms = lax.dot_general(
        jnp.concatenate(lefts, axis=0),
        jnp.concatenate(grads, axis=0),
        (((0,), (0,)), ((), ())),
        preferred_element_type=F32,
    )
    return updates, terms


def mix_kernel(half, chunks, sizes, final, *refs):
    n_prev, n_now = sizes
    prevs, nows = refs[:n_prev], refs[n_prev : n_prev + n_now]
    feat_hbm, cot_hbm, v_hbm, *refs = refs[n_prev + n_now :]
    *refs, p_ref, q_ref, feat_ref, cot_ref, v_ref, up_ref, g_ref, given_ref, sems = refs
    given = refs[0] if half == 0 else None
    up_hbm, outs = refs[-2 - final], refs[-1 - final :]
    rows, count = MIX_ROWS, len(chunks)
    pair = slice(2 * half, 2 * half + 2)
    first = pltpu.make_async_copy(v_hbm, v_ref, sems.at[0])
    last = pltpu.make_async_copy(given, given_ref, sems.at[1]) if given is not None else None
    loads, stores = [], []
    for c, (p, p_row, q, q_row, place) in enumerate(chunks):
        here, there = slice(c * rows, (c + 1) * rows), slice(place, place + rows)
        moves = (
            (nows[q].at[:, q_row : q_row + rows], q_ref),
            (prevs[p].at[:, p_row : p_row + rows], p_ref),
            (feat_hbm.at[pair, there], feat_ref),
            (cot_hbm.at[pair, there], cot_ref),
        )
        loads.append(
            [
                pltpu.make_async_copy(src, dst.at[:, here], sems.at[2 + 5 * c + i])
                for i, (src, dst) in enumerate(moves)
            ]
        )
        stores.append(
            pltpu.make_async_copy(
                up_ref.at[:, here], up_hbm.at[pair, there], sems.at[2 + 5 * c + 4]
            )
        )
    first.start()
    for copy in sum(loads, []):
        copy.start()
    if last is not None:
        last.start()
    first.wait()
    for c in range(count):
        for copy in loads[c]:
            copy.wait()
        here = slice(c * rows, (c + 1) * rows)
        before = [p_ref[0, here], p_ref[1, here], q_ref[0, here], q_ref[1, here]]
        updates, terms = chunk_terms(
            before,
            [feat_ref[f, here] for f in range(2)],
            [cot_ref[f, here] for f in range(2)],
            v_ref,
        )
        for f in range(2):
            up_ref[f, here] = updates[f]
        stores[c].start()
        g_ref[...] = terms if c == 0 else g_ref[...] + terms
    if last is not None:
        last.wait()
    if final:
        me = refs[1][0]
        share = g_ref.shape[0] // 2
        low, high = slice(0, share), slice(share, 2 * share)
        for core, (mine, theirs) in enumerate(((low, high), (high, low))):

            @pl.when(me == core)
            def _(mine=mine, theirs=theirs):
                outs[0][...] = g_ref[mine] + given_ref[mine]
                outs[1][...] = g_ref[theirs] + given_ref[theirs]

    else:
        outs[0][...] = g_ref[...] + given_ref[...] if last is not None else g_ref[...]
    for copy in stores:
        copy.wait()


def mix(half, chunks, prevs, nows, features, cotangent, v, given=None, me=None):
    frames, width = 2, v.shape[1]
    anywhere = pl.BlockSpec(memory_space=pl.ANY)
    block = pltpu.VMEM((frames, len(chunks) * MIX_ROWS, width), BF16)
    sums = jax.ShapeDtypeStruct(v.shape, F32)
    share = jax.ShapeDtypeStruct((v.shape[0] // 2, width), F32)
    arrays = [*prevs, *nows, features, cotangent, v]
    specs = [anywhere] * len(arrays)
    aliases = {}
    if given is not None:
        final = 1 if me is not None else 0
        total, updated = given
        core = me if final else jnp.zeros((1,), jnp.int32)
        arrays += [total, core, updated]
        aliases = {len(arrays) - 1: 0}
        specs += [anywhere, pl.BlockSpec(memory_space=pltpu.SMEM), anywhere]
    else:
        final = 0
    return pl.pallas_call(
        functools.partial(mix_kernel, half, chunks, (len(prevs), len(nows)), final),
        in_specs=specs,
        out_specs=[anywhere] + [whole_vmem()] * (1 + final),
        out_shape=[jax.ShapeDtypeStruct(features.shape, BF16)]
        + ([share, share] if final else [sums]),
        scratch_shapes=[block] * 4
        + [
            pltpu.VMEM(v.shape, BF16),
            block,
            pltpu.VMEM(v.shape, F32),
            pltpu.VMEM(v.shape, F32),
            pltpu.SemaphoreType.DMA((2 + 5 * len(chunks),)),
        ],
        input_output_aliases=aliases,
        compiler_params=pltpu.CompilerParams(vmem_limit_bytes=VMEM),
        cost_estimate=pl.CostEstimate(flops=1, bytes_accessed=1, transcendentals=0),
        name="mix",
    )(*arrays)


def middle_kernel(row, codes, feat, *refs):
    ins, scratch = refs[:16], refs[16:]
    halo, mask_hbm, nows = ins[:6], ins[6], ins[7:10]
    prev_hbm, flat_hbm, cot_hbm, v_hbm, agg_hbm, up_hbm = ins[10:]
    g_out, ext, mask_ref, agg_ref, q_ref, p_ref, feat_ref, cot_ref, up_ref, v_ref, sems = scratch
    _, nx, ny, lipids, _ = feat.shape
    count, rows = nx * ny * lipids, MIX_ROWS
    end = count - row
    used = [0]

    def copy(src, dst):
        used[0] += 1
        return pltpu.make_async_copy(src, dst, sems.at[used[0] - 1])

    groups = []
    for f in range(2):
        moves = [
            copy(feat.at[f], ext.at[f, 1 : nx + 1, 1 : ny + 1]),
            copy(halo[0].at[f], ext.at[f, 1 : nx + 1, 0:1]),
            copy(halo[1].at[f], ext.at[f, 1 : nx + 1, ny + 1 : ny + 2]),
            copy(halo[2].at[f], ext.at[f, 0:1, 1 : ny + 1]),
            copy(halo[3].at[f], ext.at[f, nx + 1 : nx + 2, 1 : ny + 1]),
            copy(halo[4].at[f, 0:1], ext.at[f, 0:1, 0:1]),
            copy(halo[4].at[f, 1:2], ext.at[f, nx + 1 : nx + 2, 0:1]),
            copy(halo[5].at[f, 0:1], ext.at[f, 0:1, ny + 1 : ny + 2]),
            copy(halo[5].at[f, 1:2], ext.at[f, nx + 1 : nx + 2, ny + 1 : ny + 2]),
        ]
        groups.append(moves)
    masks = [
        copy(mask_hbm.at[x * ny : (x + 1) * ny], mask_ref.at[x * ny : (x + 1) * ny])
        for x in range(nx)
    ]
    load_v = copy(v_hbm, v_ref)
    work, slot = [], 0
    for half, first, last in ((1, 0, count), (0, row, end)):
        pair = slice(2 * half, 2 * half + 2)
        for r in range(first, last, rows):
            there, here = slice(r, r + rows), slice(slot, slot + rows)
            slot += rows
            if half:
                n, at = (1, r) if r < row else ((0, r - row) if r < end else (2, r - end))
                moves = [copy(nows[n].at[:, at : at + rows], q_ref.at[:, there])]
            else:
                at = slice(r - row, r - row + rows)
                moves = [copy(prev_hbm.at[:, at], p_ref.at[:, at])]
            moves.append(copy(cot_hbm.at[pair, there], cot_ref.at[:, here]))
            if half:
                moves.append(copy(flat_hbm.at[pair, there], feat_ref.at[:, there]))
            store = copy(up_ref.at[:, here], up_hbm.at[pair, there])
            work.append((half, r, here, moves, store))
    sent = [copy(agg_ref.at[f], agg_hbm.at[f]) for f in range(2)]
    for moves in (groups[0], masks, groups[1]):
        for move in moves:
            move.start()
    load_v.start()
    for item in work:
        for move in item[3]:
            move.start()
    slots = mask_ref.shape[2] // lipids
    for f in range(2):
        for move in groups[f]:
            move.wait()
        for x in range(nx):
            if f == 0:
                masks[x].wait()
            for y in range(ny):
                tile = x * ny + y
                parts = []
                for k in range(slots):
                    code = codes[tile * slots + k]
                    parts.append(ext[f, x + lax.div(code, 3), y + lax.rem(code, 3)])
                summed = jnp.dot(
                    mask_ref[tile],
                    jnp.concatenate(parts, axis=0),
                    preferred_element_type=F32,
                )
                agg_ref[f, tile * lipids : (tile + 1) * lipids] = (0.18 * summed).astype(BF16)
        sent[f].start()
    load_v.wait()
    for n, (half, r, here, moves, store) in enumerate(work):
        for move in moves:
            move.wait()
        there = slice(r, r + rows)
        mid = [agg_ref[0, there], agg_ref[1, there]]
        if half:
            before = mid + [q_ref[0, there], q_ref[1, there]]
            own = [feat_ref[f, there] for f in range(2)]
        else:
            tiles = [divmod(t // lipids, ny) for t in range(r, r + rows, lipids)]
            own = [
                jnp.concatenate([ext[f, x + 1, y + 1] for x, y in tiles], axis=0)
                for f in range(2)
            ]
            at = slice(r - row, r - row + rows)
            before = [p_ref[0, at], p_ref[1, at]] + mid
        updates, terms = chunk_terms(
            before, own, [cot_ref[f, here] for f in range(2)], v_ref
        )
        for f in range(2):
            up_ref[f, here] = updates[f]
        store.start()
        g_out[...] = terms if n == 0 else g_out[...] + terms
    for move in sent:
        move.wait()
    for item in work:
        item[4].wait()


def middle(row, codes, features, halo, mask, nows, prev, cotangent, v):
    frames, nx, ny, lipids, width = features.shape
    count = nx * ny * lipids
    flat = (frames, count, width)
    anywhere = pl.BlockSpec(memory_space=pl.ANY)
    some = 2 * count - 2 * row
    chunks = some // MIX_ROWS
    return pl.pallas_call(
        functools.partial(middle_kernel, row),
        in_specs=[pl.BlockSpec(memory_space=pltpu.SMEM)] + [anywhere] * 15,
        out_specs=[anywhere, anywhere, whole_vmem()],
        out_shape=[
            jax.ShapeDtypeStruct((2, count, width), BF16),
            jax.ShapeDtypeStruct(flat, BF16),
            jax.ShapeDtypeStruct(v.shape, F32),
        ],
        scratch_shapes=[
            pltpu.VMEM((2, nx + 2, ny + 2, lipids, width), BF16),
            pltpu.VMEM(mask.shape, BF16),
            pltpu.VMEM((2, count, width), BF16),
            pltpu.VMEM((2, count, width), BF16),
            pltpu.VMEM((2, count - 2 * row, width), BF16),
            pltpu.VMEM((2, count, width), BF16),
            pltpu.VMEM((2, some, width), BF16),
            pltpu.VMEM((2, some, width), BF16),
            pltpu.VMEM(v.shape, BF16),
            pltpu.SemaphoreType.DMA((25 + 4 * chunks,)),
        ],
        compiler_params=pltpu.CompilerParams(vmem_limit_bytes=VMEM),
        cost_estimate=pl.CostEstimate(flops=1, bytes_accessed=1, transcendentals=0),
        name="middle",
    )(
        codes,
        features,
        *halo,
        mask,
        *nows,
        prev,
        features.reshape(flat),
        cotangent,
        v,
    )


def finish_kernel(scale, g_ref, ws_ref, wt_ref, space_ref, time_ref):
    width = ws_ref.shape[0]
    space = jnp.zeros((width, width), F32)
    for j in range(wt_ref.shape[0]):
        g = g_ref[j * width : (j + 1) * width, :]
        high = g.astype(BF16)
        low = (g - high.astype(F32)).astype(BF16)
        time = 0.0
        for part in (low, high):
            time = time + lax.dot_general(
                ws_ref[...], part, (((0,), (0,)), ((), ())), preferred_element_type=F32
            )
            space = space + lax.dot_general(
                part, wt_ref[j], (((1,), (1,)), ((), ())), preferred_element_type=F32
            )
        time_ref[j] = time * scale
    space_ref[...] = space * scale


def finish(scale, total, w_space, w_time):
    return pl.pallas_call(
        functools.partial(finish_kernel, scale),
        in_specs=[whole_vmem()] * 3,
        out_specs=[whole_vmem()] * 2,
        out_shape=[
            jax.ShapeDtypeStruct(w_space.shape, F32),
            jax.ShapeDtypeStruct(w_time.shape, F32),
        ],
        compiler_params=pltpu.CompilerParams(vmem_limit_bytes=20 << 20),
        name="finish",
    )(total, w_space, w_time)


def all_sum(keep, give):
    half, width = keep.shape
    block, count = 8, lax.axis_size(REST)
    mine = keep + lax.ppermute(give, "core", ring(2, 1))
    mine = jnp.pad(mine, ((0, count * block - half), (0, 0)))
    mine = lax.all_to_all(mine.reshape(count, block, width), REST, 0, 0, tiled=True)
    spread = jnp.broadcast_to(mine.sum(axis=0)[None], (count, block, width))
    back = lax.all_to_all(spread, REST, 0, 0, tiled=True)
    back = back.reshape(count * block, width)[:half]
    other = lax.ppermute(back, "core", ring(2, 1))
    first = lax.axis_index("core") == 0
    return jnp.where(
        first, jnp.concatenate([back, other]), jnp.concatenate([other, back])
    )


def shards(features, neighbours, adjacency, w_space, w_time, cotangent):
    frames, nx, ny, lipids, width = features.shape
    count = nx * ny * lipids
    codes = neighbours.reshape(-1)
    up, down = ring(4, 1), ring(4, -1)
    onward = [(i, i + 1) for i in range(7)]
    inner, outer = tuple(range(1, nx - 1)), (0, nx - 1)

    every = slice(None)
    low, high = slice(0, 1), slice(ny - 1, ny)

    def exchange(axis, high_edge, low_edge):
        return lax.ppermute(high_edge, axis, up), lax.ppermute(low_edge, axis, down)

    def y_edges(first, source):
        edge = (2, nx, 1, lipids, width)
        pair = slice(first, first + 2)
        moves = [(0, (pair, every, side), o, ()) for o, side in enumerate((high, low))]
        return pack([source], [edge, edge], moves)

    def corner_edges(x_halo):
        corner = (2, 2, 1, lipids, width)
        moves = [
            (i, (slice(2 * p, 2 * p + 2), every, side), 2 * p + o, (every, slice(i, i + 1)))
            for i in range(2)
            for p in range(2)
            for o, side in enumerate((high, low))
        ]
        return pack(x_halo, [corner] * 4, moves)

    edges_x = (features[:, nx - 1 :], features[:, :1])
    x_halo = exchange(GX, *edges_x)
    later, _ = lax.optimization_barrier((features, edges_x))
    edges_b = y_edges(2, later)
    y_b = exchange("gy", *edges_b)
    contacts = adjacency.reshape(nx * ny, -1, lipids, lipids)
    contacts, _ = lax.optimization_barrier((contacts, edges_b))
    mask, v = prep(contacts, w_space, w_time)
    later, _ = lax.optimization_barrier((features, mask))
    edges_a = y_edges(0, later)
    y_a = exchange("gy", *edges_a)
    (inner_b,) = aggregate(2, inner, codes, features, y_b, mask)
    x_halo, sent = lax.optimization_barrier((x_halo, inner_b))
    prev_inner = lax.ppermute(sent, "ta", onward)
    ends = corner_edges(x_halo)
    c_b = exchange("gy", *ends[2:])
    c_a = exchange("gy", *ends[:2])
    c_b, y_a = lax.optimization_barrier((c_b, y_a))
    outer_b = aggregate(2, outer, codes, features, (*y_b, *x_halo, *c_b), mask, 2)
    c_a, sent = lax.optimization_barrier((c_a, outer_b))
    prev_first = lax.ppermute(sent[0], "ta", onward)
    prev_last = lax.ppermute(sent[1], "ta", onward)
    feat = features.reshape(frames, count, width)
    cot = cotangent.reshape(frames, count, width)
    a_row = ny * lipids
    end = count - a_row
    agg_a, updated, total = middle(
        a_row,
        codes,
        features,
        (*y_a, *x_halo, *c_a),
        mask,
        (inner_b, *outer_b),
        prev_inner,
        cot,
        v,
    )
    updated, total = mix(
        0,
        [(0, r, 0, r, r) for r in range(0, a_row, MIX_ROWS)],
        [prev_first],
        [agg_a],
        feat,
        cot,
        v,
        (total, updated),
    )
    me = lax.axis_index("core").reshape(1)
    updated, keep, give = mix(
        0,
        [(0, r - end, 0, r, r) for r in range(end, count, MIX_ROWS)],
        [prev_last],
        [agg_a],
        feat,
        cot,
        v,
        (total, updated),
        me,
    )
    total = all_sum(keep, give)
    scale = 1.0 / math.sqrt(frames * count * lax.axis_size(EVERY))
    grad_space, grad_time = finish(scale, total, w_space, w_time)
    return updated.reshape(features.shape), grad_space, grad_time


def solution(mesh):
    gx, gy, ta = (mesh.shape[a] for a in ("gx", "gy", "ta"))
    fine = Mesh(
        np.asarray(mesh.devices).reshape(2, gx // 2, gy, ta), ("yh", "core", "gy", "ta")
    )
    in_specs = (
        P("ta", GX, "gy", None, None),
        P(GX, "gy", None),
        P(GX, "gy", None, None, None),
        P(),
        P(),
        P("ta", GX, "gy", None, None),
    )
    out_specs = (P("ta", GX, "gy", None, None), P(), P())
    return jax.shard_map(shards, mesh=fine, in_specs=in_specs, out_specs=out_specs, check_vma=False)
```

```python
import functools
import math

import jax
import jax.numpy as jnp
import numpy as np
from jax import lax
from jax.experimental import pallas as pl
from jax.experimental.pallas import tpu as pltpu
from jax.sharding import Mesh
from jax.sharding import PartitionSpec as P

BF16 = jnp.bfloat16
F32 = jnp.float32
GX = ("yh", "core")
MIX_ROWS = 512
VMEM = 65300 << 10
EVERY = ("yh", "core", "gy", "ta")
REST = ("yh", "gy", "ta")


def ring(count, step):
    return [(i, (i + step) % count) for i in range(count)]


def whole_vmem():
    return pl.BlockSpec(memory_space=pltpu.VMEM)


def prep_kernel(adj_ref, ws_ref, wt_ref, mask_ref, v_ref):
    slots, lipids = adj_ref.shape[1], adj_ref.shape[2]
    width = ws_ref.shape[1]
    for t in range(adj_ref.shape[0]):
        for k in range(slots):
            mask_ref[t, :, k * lipids : (k + 1) * lipids] = (
                adj_ref[t, k].astype(F32).astype(BF16)
            )

    @pl.when(pl.program_id(0) == 0)
    def _():
        for j in range(wt_ref.shape[0]):
            v_ref[j * width : (j + 1) * width, :] = jnp.dot(
                ws_ref[...], wt_ref[j], preferred_element_type=F32
            ).astype(BF16)


def prep(adjacency, w_space, w_time):
    tiles, slots, lipids, _ = adjacency.shape
    taps, width, _ = w_time.shape
    return pl.pallas_call(
        prep_kernel,
        grid=(tiles // 4,),
        in_specs=[
            pl.BlockSpec((4, slots, lipids, lipids), lambda i: (i, 0, 0, 0)),
            pl.BlockSpec((width, width), lambda i: (0, 0)),
            pl.BlockSpec((taps, width, width), lambda i: (0, 0, 0)),
        ],
        out_specs=[
            pl.BlockSpec((4, lipids, slots * lipids), lambda i: (i, 0, 0)),
            pl.BlockSpec((taps * width, width), lambda i: (0, 0)),
        ],
        out_shape=[
            jax.ShapeDtypeStruct((tiles, lipids, slots * lipids), BF16),
            jax.ShapeDtypeStruct((taps * width, width), BF16),
        ],
        compiler_params=pltpu.CompilerParams(vmem_limit_bytes=VMEM),
        cost_estimate=pl.CostEstimate(
            flops=2 * taps * width**3, bytes_accessed=8 << 20, transcendentals=0
        ),
        name="prep",
    )(adjacency, w_space, w_time)


def pack_kernel(moves, count, *refs):
    *arrays, sems = refs
    copies = [
        pltpu.make_async_copy(arrays[i].at[src], arrays[count + o].at[dst], sems.at[n])
        for n, (i, src, o, dst) in enumerate(moves)
    ]
    for copy in copies:
        copy.start()
    for copy in copies:
        copy.wait()


def pack(arrays, shapes, moves):
    anywhere = pl.BlockSpec(memory_space=pl.ANY)
    return pl.pallas_call(
        functools.partial(pack_kernel, moves, len(arrays)),
        in_specs=[anywhere] * len(arrays),
        out_specs=[whole_vmem()] * len(shapes),
        out_shape=[jax.ShapeDtypeStruct(shape, BF16) for shape in shapes],
        scratch_shapes=[pltpu.SemaphoreType.DMA((len(moves),))],
        compiler_params=pltpu.CompilerParams(vmem_limit_bytes=VMEM),
        cost_estimate=pl.CostEstimate(flops=0, bytes_accessed=6 << 20, transcendentals=0),
        name="pack",
    )(*arrays)


def agg_kernel(first, xs, edge, pieces, codes, feat, *rest):
    *ins, ext, mask_ref, out_ref, sems = rest
    halo, mask_hbm, outs = ins[: -pieces - 1], ins[-pieces - 1], ins[-pieces:]
    frames, _, ny = out_ref.shape[:3]
    nx = feat.shape[1]
    inside = slice(edge, nx + edge)
    groups = []
    for f in range(frames):
        moves = [
            (feat.at[first + f], ext.at[f, inside, 1 : ny + 1]),
            (halo[0].at[f], ext.at[f, inside, 0:1]),
            (halo[1].at[f], ext.at[f, inside, ny + 1 : ny + 2]),
        ]
        if f == 0:
            moves += [
                (mask_hbm.at[x * ny : (x + 1) * ny], mask_ref.at[i * ny : (i + 1) * ny])
                for i, x in enumerate(xs)
            ]
        if edge:
            xlo, xhi = (ref.at[first + f] for ref in halo[2:4])
            clo, chi = (ref.at[f] for ref in halo[4:])
            moves += [
                (xlo, ext.at[f, 0:1, 1 : ny + 1]),
                (xhi, ext.at[f, nx + 1 : nx + 2, 1 : ny + 1]),
                (clo.at[0:1], ext.at[f, 0:1, 0:1]),
                (clo.at[1:2], ext.at[f, nx + 1 : nx + 2, 0:1]),
                (chi.at[0:1], ext.at[f, 0:1, ny + 1 : ny + 2]),
                (chi.at[1:2], ext.at[f, nx + 1 : nx + 2, ny + 1 : ny + 2]),
            ]
        groups.append(moves)
    copies, used = [], 0
    for moves in groups:
        copies.append(
            [
                pltpu.make_async_copy(src, dst, sems.at[used + i])
                for i, (src, dst) in enumerate(moves)
            ]
        )
        used += len(moves)
        for copy in copies[-1]:
            copy.start()
    slots = mask_ref.shape[2] // mask_ref.shape[1]
    sent = []
    for f in range(frames):
        for copy in copies[f]:
            copy.wait()
        for i, x in enumerate(xs):
            for y in range(ny):
                places = []
                for k in range(slots):
                    code = codes[x, y, k]
                    places.append(
                        (x - 1 + edge + lax.div(code, 3), y + lax.rem(code, 3))
                    )
                source = jnp.concatenate([ext[f, sx, sy] for sx, sy in places], axis=0)
                summed = jnp.dot(
                    mask_ref[i * ny + y], source, preferred_element_type=F32
                )
                out_ref[f, i, y] = (0.18 * summed).astype(BF16)
        piece = len(xs) // pieces
        for n, out in enumerate(outs):
            rows = slice(n * piece, (n + 1) * piece)
            copy = pltpu.make_async_copy(
                out_ref.at[f, rows], out.at[f], sems.at[used + f * pieces + n]
            )
            copy.start()
            sent.append(copy)
    for copy in sent:
        copy.wait()


def aggregate(first, xs, codes, features, halo, mask, pieces=1):
    _, nx, ny, lipids, width = features.shape
    frames = 2
    slots = mask.shape[2] // lipids
    edge = 1 if len(halo) > 2 else 0
    anywhere = pl.BlockSpec(memory_space=pl.ANY)
    flops = 2 * frames * len(xs) * ny * lipids * mask.shape[2] * width
    out_shape = (frames, len(xs), ny, lipids, width)
    out = pl.pallas_call(
        functools.partial(agg_kernel, first, xs, edge, pieces),
        in_specs=[pl.BlockSpec(memory_space=pltpu.SMEM)] + [anywhere] * (len(halo) + 2),
        out_specs=[anywhere] * pieces,
        out_shape=[
            jax.ShapeDtypeStruct(
                (frames, len(xs) // pieces, ny, lipids, width), BF16
            )
        ]
        * pieces,
        scratch_shapes=[
            pltpu.VMEM((frames, nx + 2 * edge, ny + 2, lipids, width), BF16),
            pltpu.VMEM((len(xs) * ny, lipids, slots * lipids), BF16),
            pltpu.VMEM(out_shape, BF16),
            pltpu.SemaphoreType.DMA((frames * (12 + len(xs)),)),
        ],
        compiler_params=pltpu.CompilerParams(vmem_limit_bytes=VMEM),
        cost_estimate=pl.CostEstimate(
            flops=flops, bytes_accessed=8 << 20, transcendentals=0
        ),
        name="aggregate",
    )(codes, features, *halo, mask)
    return [piece.reshape(frames, -1, width) for piece in out]


def chunk_terms(before, features, cotangents, v_ref):
    lefts, grads, updates = [], [], []
    for f in range(2):
        left = jnp.concatenate([before[f + 2], before[f + 1], before[f]], axis=1)
        mixed = jnp.dot(left, v_ref[...], preferred_element_type=F32)
        s = 0.5 * jnp.tanh(0.5 * mixed) + 0.5
        silu = mixed * s
        updates.append((features[f].astype(F32) + silu).astype(BF16))
        grad = cotangents[f].astype(F32) * (s + silu * (1.0 - s))
        lefts.append(left)
        grads.append(grad.astype(BF16))
    terms = lax.dot_general(
        jnp.concatenate(lefts, axis=0),
        jnp.concatenate(grads, axis=0),
        (((0,), (0,)), ((), ())),
        preferred_element_type=F32,
    )
    return updates, terms


def mix_kernel(half, chunks, sizes, final, *refs):
    n_prev, n_now = sizes
    prevs, nows = refs[:n_prev], refs[n_prev : n_prev + n_now]
    feat_hbm, cot_hbm, v_hbm, *refs = refs[n_prev + n_now :]
    *refs, p_ref, q_ref, feat_ref, cot_ref, v_ref, up_ref, g_ref, given_ref, sems = refs
    given = refs[0] if half == 0 else None
    up_hbm, outs = refs[-2 - final], refs[-1 - final :]
    rows, count = MIX_ROWS, len(chunks)
    pair = slice(2 * half, 2 * half + 2)
    first = pltpu.make_async_copy(v_hbm, v_ref, sems.at[0])
    last = pltpu.make_async_copy(given, given_ref, sems.at[1]) if given is not None else None
    loads, stores = [], []
    for c, (p, p_row, q, q_row, place) in enumerate(chunks):
        here, there = slice(c * rows, (c + 1) * rows), slice(place, place + rows)
        moves = (
            (nows[q].at[:, q_row : q_row + rows], q_ref),
            (prevs[p].at[:, p_row : p_row + rows], p_ref),
            (feat_hbm.at[pair, there], feat_ref),
            (cot_hbm.at[pair, there], cot_ref),
        )
        loads.append(
            [
                pltpu.make_async_copy(src, dst.at[:, here], sems.at[2 + 5 * c + i])
                for i, (src, dst) in enumerate(moves)
            ]
        )
        stores.append(
            pltpu.make_async_copy(
                up_ref.at[:, here], up_hbm.at[pair, there], sems.at[2 + 5 * c + 4]
            )
        )
    first.start()
    for copy in sum(loads, []):
        copy.start()
    if last is not None:
        last.start()
    first.wait()
    for c in range(count):
        for copy in loads[c]:
            copy.wait()
        here = slice(c * rows, (c + 1) * rows)
        before = [p_ref[0, here], p_ref[1, here], q_ref[0, here], q_ref[1, here]]
        updates, terms = chunk_terms(
            before,
            [feat_ref[f, here] for f in range(2)],
            [cot_ref[f, here] for f in range(2)],
            v_ref,
        )
        for f in range(2):
            up_ref[f, here] = updates[f]
        stores[c].start()
        g_ref[...] = terms if c == 0 else g_ref[...] + terms
    if last is not None:
        last.wait()
    if final:
        me = refs[1][0]
        share = g_ref.shape[0] // 2
        low, high = slice(0, share), slice(share, 2 * share)
        for core, (mine, theirs) in enumerate(((low, high), (high, low))):

            @pl.when(me == core)
            def _(mine=mine, theirs=theirs):
                outs[0][...] = g_ref[mine] + given_ref[mine]
                outs[1][...] = g_ref[theirs] + given_ref[theirs]

    else:
        outs[0][...] = g_ref[...] + given_ref[...] if last is not None else g_ref[...]
    for copy in stores:
        copy.wait()


def mix(half, chunks, prevs, nows, features, cotangent, v, given=None, me=None):
    frames, width = 2, v.shape[1]
    anywhere = pl.BlockSpec(memory_space=pl.ANY)
    block = pltpu.VMEM((frames, len(chunks) * MIX_ROWS, width), BF16)
    sums = jax.ShapeDtypeStruct(v.shape, F32)
    share = jax.ShapeDtypeStruct((v.shape[0] // 2, width), F32)
    arrays = [*prevs, *nows, features, cotangent, v]
    specs = [anywhere] * len(arrays)
    aliases = {}
    if given is not None:
        final = 1 if me is not None else 0
        total, updated = given
        core = me if final else jnp.zeros((1,), jnp.int32)
        arrays += [total, core, updated]
        aliases = {len(arrays) - 1: 0}
        specs += [anywhere, pl.BlockSpec(memory_space=pltpu.SMEM), anywhere]
    else:
        final = 0
    return pl.pallas_call(
        functools.partial(mix_kernel, half, chunks, (len(prevs), len(nows)), final),
        in_specs=specs,
        out_specs=[anywhere] + [whole_vmem()] * (1 + final),
        out_shape=[jax.ShapeDtypeStruct(features.shape, BF16)]
        + ([share, share] if final else [sums]),
        scratch_shapes=[block] * 4
        + [
            pltpu.VMEM(v.shape, BF16),
            block,
            pltpu.VMEM(v.shape, F32),
            pltpu.VMEM(v.shape, F32),
            pltpu.SemaphoreType.DMA((2 + 5 * len(chunks),)),
        ],
        input_output_aliases=aliases,
        compiler_params=pltpu.CompilerParams(vmem_limit_bytes=VMEM),
        cost_estimate=pl.CostEstimate(flops=1, bytes_accessed=1, transcendentals=0),
        name="mix",
    )(*arrays)


def middle_kernel(row, codes, feat, *refs):
    ins, scratch = refs[:16], refs[16:]
    halo, mask_hbm, nows = ins[:6], ins[6], ins[7:10]
    prev_hbm, flat_hbm, cot_hbm, v_hbm, agg_hbm, up_hbm = ins[10:]
    g_out, ext, mask_ref, agg_ref, q_ref, p_ref, feat_ref, cot_ref, up_ref, v_ref, sems = scratch
    _, nx, ny, lipids, _ = feat.shape
    count, rows = nx * ny * lipids, MIX_ROWS
    end = count - row
    used = [0]

    def copy(src, dst):
        used[0] += 1
        return pltpu.make_async_copy(src, dst, sems.at[used[0] - 1])

    groups = []
    for f in range(2):
        moves = [
            copy(feat.at[f], ext.at[f, 1 : nx + 1, 1 : ny + 1]),
            copy(halo[0].at[f], ext.at[f, 1 : nx + 1, 0:1]),
            copy(halo[1].at[f], ext.at[f, 1 : nx + 1, ny + 1 : ny + 2]),
            copy(halo[2].at[f], ext.at[f, 0:1, 1 : ny + 1]),
            copy(halo[3].at[f], ext.at[f, nx + 1 : nx + 2, 1 : ny + 1]),
            copy(halo[4].at[f, 0:1], ext.at[f, 0:1, 0:1]),
            copy(halo[4].at[f, 1:2], ext.at[f, nx + 1 : nx + 2, 0:1]),
            copy(halo[5].at[f, 0:1], ext.at[f, 0:1, ny + 1 : ny + 2]),
            copy(halo[5].at[f, 1:2], ext.at[f, nx + 1 : nx + 2, ny + 1 : ny + 2]),
        ]
        groups.append(moves)
    masks = [
        copy(mask_hbm.at[x * ny : (x + 1) * ny], mask_ref.at[x * ny : (x + 1) * ny])
        for x in range(nx)
    ]
    load_v = copy(v_hbm, v_ref)
    work, slot = [], 0
    for half, first, last in ((1, 0, count), (0, row, end)):
        pair = slice(2 * half, 2 * half + 2)
        for r in range(first, last, rows):
            there, here = slice(r, r + rows), slice(slot, slot + rows)
            slot += rows
            if half:
                n, at = (1, r) if r < row else ((0, r - row) if r < end else (2, r - end))
                moves = [copy(nows[n].at[:, at : at + rows], q_ref.at[:, there])]
            else:
                at = slice(r - row, r - row + rows)
                moves = [copy(prev_hbm.at[:, at], p_ref.at[:, at])]
            moves.append(copy(cot_hbm.at[pair, there], cot_ref.at[:, here]))
            if half:
                moves.append(copy(flat_hbm.at[pair, there], feat_ref.at[:, there]))
            store = copy(up_ref.at[:, here], up_hbm.at[pair, there])
            work.append((half, r, here, moves, store))
    sent = [copy(agg_ref.at[f], agg_hbm.at[f]) for f in range(2)]
    for moves in (groups[0], masks, groups[1]):
        for move in moves:
            move.start()
    load_v.start()
    for item in work:
        for move in item[3]:
            move.start()
    slots = mask_ref.shape[2] // lipids
    for f in range(2):
        for move in groups[f]:
            move.wait()
        for x in range(nx):
            if f == 0:
                masks[x].wait()
            for y in range(ny):
                tile = x * ny + y
                parts = []
                for k in range(slots):
                    code = codes[x, y, k]
                    parts.append(ext[f, x + lax.div(code, 3), y + lax.rem(code, 3)])
                summed = jnp.dot(
                    mask_ref[tile],
                    jnp.concatenate(parts, axis=0),
                    preferred_element_type=F32,
                )
                agg_ref[f, tile * lipids : (tile + 1) * lipids] = (0.18 * summed).astype(BF16)
        sent[f].start()
    load_v.wait()
    for n, (half, r, here, moves, store) in enumerate(work):
        for move in moves:
            move.wait()
        there = slice(r, r + rows)
        mid = [agg_ref[0, there], agg_ref[1, there]]
        if half:
            before = mid + [q_ref[0, there], q_ref[1, there]]
            own = [feat_ref[f, there] for f in range(2)]
        else:
            tiles = [divmod(t // lipids, ny) for t in range(r, r + rows, lipids)]
            own = [
                jnp.concatenate([ext[f, x + 1, y + 1] for x, y in tiles], axis=0)
                for f in range(2)
            ]
            at = slice(r - row, r - row + rows)
            before = [p_ref[0, at], p_ref[1, at]] + mid
        updates, terms = chunk_terms(
            before, own, [cot_ref[f, here] for f in range(2)], v_ref
        )
        for f in range(2):
            up_ref[f, here] = updates[f]
        store.start()
        g_out[...] = terms if n == 0 else g_out[...] + terms
    for move in sent:
        move.wait()
    for item in work:
        item[4].wait()


def middle(row, codes, features, halo, mask, nows, prev, cotangent, v):
    frames, nx, ny, lipids, width = features.shape
    count = nx * ny * lipids
    flat = (frames, count, width)
    anywhere = pl.BlockSpec(memory_space=pl.ANY)
    some = 2 * count - 2 * row
    chunks = some // MIX_ROWS
    return pl.pallas_call(
        functools.partial(middle_kernel, row),
        in_specs=[pl.BlockSpec(memory_space=pltpu.SMEM)] + [anywhere] * 15,
        out_specs=[anywhere, anywhere, whole_vmem()],
        out_shape=[
            jax.ShapeDtypeStruct((2, count, width), BF16),
            jax.ShapeDtypeStruct(flat, BF16),
            jax.ShapeDtypeStruct(v.shape, F32),
        ],
        scratch_shapes=[
            pltpu.VMEM((2, nx + 2, ny + 2, lipids, width), BF16),
            pltpu.VMEM(mask.shape, BF16),
            pltpu.VMEM((2, count, width), BF16),
            pltpu.VMEM((2, count, width), BF16),
            pltpu.VMEM((2, count - 2 * row, width), BF16),
            pltpu.VMEM((2, count, width), BF16),
            pltpu.VMEM((2, some, width), BF16),
            pltpu.VMEM((2, some, width), BF16),
            pltpu.VMEM(v.shape, BF16),
            pltpu.SemaphoreType.DMA((25 + 4 * chunks,)),
        ],
        compiler_params=pltpu.CompilerParams(vmem_limit_bytes=VMEM),
        cost_estimate=pl.CostEstimate(flops=1, bytes_accessed=1, transcendentals=0),
        name="middle",
    )(
        codes,
        features,
        *halo,
        mask,
        *nows,
        prev,
        features.reshape(flat),
        cotangent,
        v,
    )


def finish_kernel(scale, g_ref, ws_ref, wt_ref, space_ref, time_ref):
    width = ws_ref.shape[0]
    space = jnp.zeros((width, width), F32)
    for j in range(wt_ref.shape[0]):
        g = g_ref[j * width : (j + 1) * width, :]
        high = g.astype(BF16)
        low = (g - high.astype(F32)).astype(BF16)
        time = 0.0
        for part in (low, high):
            time = time + lax.dot_general(
                ws_ref[...], part, (((0,), (0,)), ((), ())), preferred_element_type=F32
            )
            space = space + lax.dot_general(
                part, wt_ref[j], (((1,), (1,)), ((), ())), preferred_element_type=F32
            )
        time_ref[j] = time * scale
    space_ref[...] = space * scale


def finish(scale, total, w_space, w_time):
    return pl.pallas_call(
        functools.partial(finish_kernel, scale),
        in_specs=[whole_vmem()] * 3,
        out_specs=[whole_vmem()] * 2,
        out_shape=[
            jax.ShapeDtypeStruct(w_space.shape, F32),
            jax.ShapeDtypeStruct(w_time.shape, F32),
        ],
        compiler_params=pltpu.CompilerParams(vmem_limit_bytes=20 << 20),
        name="finish",
    )(total, w_space, w_time)


def all_sum(keep, give):
    half, width = keep.shape
    block, count = 8, lax.axis_size(REST)
    mine = keep + lax.ppermute(give, "core", ring(2, 1))
    mine = jnp.pad(mine, ((0, count * block - half), (0, 0)))
    mine = lax.all_to_all(mine.reshape(count, block, width), REST, 0, 0, tiled=True)
    spread = jnp.broadcast_to(mine.sum(axis=0)[None], (count, block, width))
    back = lax.all_to_all(spread, REST, 0, 0, tiled=True)
    back = back.reshape(count * block, width)[:half]
    other = lax.ppermute(back, "core", ring(2, 1))
    first = lax.axis_index("core") == 0
    return jnp.where(
        first, jnp.concatenate([back, other]), jnp.concatenate([other, back])
    )


def shards(features, neighbours, adjacency, w_space, w_time, cotangent):
    frames, nx, ny, lipids, width = features.shape
    count = nx * ny * lipids
    codes = neighbours
    up, down = ring(4, 1), ring(4, -1)
    onward = [(i, i + 1) for i in range(7)]
    inner, outer = tuple(range(1, nx - 1)), (0, nx - 1)

    every = slice(None)
    low, high = slice(0, 1), slice(ny - 1, ny)

    def exchange(axis, high_edge, low_edge):
        return lax.ppermute(high_edge, axis, up), lax.ppermute(low_edge, axis, down)

    def x_edges(source):
        edge = (frames, 1, ny, lipids, width)
        moves = [(0, (every, slice(nx - 1, nx)), 0, ()), (0, (every, low), 1, ())]
        return pack([source], [edge, edge], moves)

    def y_edges(first, source):
        edge = (2, nx, 1, lipids, width)
        pair = slice(first, first + 2)
        moves = [(0, (pair, every, side), o, ()) for o, side in enumerate((high, low))]
        return pack([source], [edge, edge], moves)

    def corner_edges(x_halo):
        corner = (2, 2, 1, lipids, width)
        moves = [
            (i, (slice(2 * p, 2 * p + 2), every, side), 2 * p + o, (every, slice(i, i + 1)))
            for i in range(2)
            for p in range(2)
            for o, side in enumerate((high, low))
        ]
        return pack(x_halo, [corner] * 4, moves)

    edges_x = x_edges(features)
    x_halo = exchange(GX, *edges_x)
    later, _ = lax.optimization_barrier((features, edges_x))
    edges_b = y_edges(2, later)
    y_b = exchange("gy", *edges_b)
    contacts = adjacency.reshape(nx * ny, -1, lipids, lipids)
    contacts, _ = lax.optimization_barrier((contacts, edges_b))
    mask, v = prep(contacts, w_space, w_time)
    later, _ = lax.optimization_barrier((features, mask))
    edges_a = y_edges(0, later)
    y_a = exchange("gy", *edges_a)
    (inner_b,) = aggregate(2, inner, codes, features, y_b, mask)
    x_halo, sent = lax.optimization_barrier((x_halo, inner_b))
    prev_inner = lax.ppermute(sent, "ta", onward)
    ends = corner_edges(x_halo)
    c_b = exchange("gy", *ends[2:])
    c_a = exchange("gy", *ends[:2])
    c_b, y_a = lax.optimization_barrier((c_b, y_a))
    outer_b = aggregate(2, outer, codes, features, (*y_b, *x_halo, *c_b), mask, 2)
    c_a, sent = lax.optimization_barrier((c_a, outer_b))
    prev_first = lax.ppermute(sent[0], "ta", onward)
    prev_last = lax.ppermute(sent[1], "ta", onward)
    feat = features.reshape(frames, count, width)
    cot = cotangent.reshape(frames, count, width)
    a_row = ny * lipids
    end = count - a_row
    agg_a, updated, total = middle(
        a_row,
        codes,
        features,
        (*y_a, *x_halo, *c_a),
        mask,
        (inner_b, *outer_b),
        prev_inner,
        cot,
        v,
    )
    updated, total = mix(
        0,
        [(0, r, 0, r, r) for r in range(0, a_row, MIX_ROWS)],
        [prev_first],
        [agg_a],
        feat,
        cot,
        v,
        (total, updated),
    )
    me = lax.axis_index("core").reshape(1)
    updated, keep, give = mix(
        0,
        [(0, r - end, 0, r, r) for r in range(end, count, MIX_ROWS)],
        [prev_last],
        [agg_a],
        feat,
        cot,
        v,
        (total, updated),
        me,
    )
    total = all_sum(keep, give)
    scale = 1.0 / math.sqrt(frames * count * lax.axis_size(EVERY))
    grad_space, grad_time = finish(scale, total, w_space, w_time)
    return updated.reshape(features.shape), grad_space, grad_time


def solution(mesh):
    gx, gy, ta = (mesh.shape[a] for a in ("gx", "gy", "ta"))
    fine = Mesh(
        np.asarray(mesh.devices).reshape(2, gx // 2, gy, ta), ("yh", "core", "gy", "ta")
    )
    in_specs = (
        P("ta", GX, "gy", None, None),
        P(GX, "gy", None),
        P(GX, "gy", None, None, None),
        P(),
        P(),
        P("ta", GX, "gy", None, None),
    )
    out_specs = (P("ta", GX, "gy", None, None), P(), P())
    return jax.shard_map(shards, mesh=fine, in_specs=in_specs, out_specs=out_specs, check_vma=False)
```
